512 devices in a mesh: seq: 64 (over x, z), exp: 8 (over y, core).
Axes of the slice: x: 4, y: 4, z: 16, core: 2. Of those that a mesh axis runs over, the one named last changes fastest.
Arguments:
- queries: bfloat16 [4096, 6144], P('seq', 'exp'), may hold values from -6 to 6
- keys: bfloat16 [4096, 6144], P('seq', 'exp'), may hold values from -6 to 6
- values: bfloat16 [4096, 6144], P('seq', 'exp'), may hold values from -6 to 6
- log_decay: float32 [48, 4096], P('exp', 'seq'), may hold values from -1 to 0
- state_in: float32 [48, 128, 128], P('exp'), may hold values from -24 to 24
- norm_gain: float32 [6144], replicated, may hold values from 0.1 to 1.9
- routes: int32 [4096, 2], P('seq'), may hold values from 0 to 7, all different within a row; in each aligned block of 64 rows (0 to 63, 64 to 127, ...) at most 20 rows name the same one
- w_gate: bfloat16 [8, 9216, 6144], P('exp', 'seq'), may hold values from -0.078125 to 0.078125
- w_up: bfloat16 [8, 9216, 6144], P('exp', 'seq'), may hold values from -0.078125 to 0.078125
Outputs:
- expert_hidden: bfloat16 [8, 9216, 1280], P('exp', 'seq')
- state_out: float32 [48, 128, 128], P('exp', 'seq')
The draws below stay inside these ranges and needn't reach their ends.
Inputs may be any that keep to these rules, and one draw needn't show every extreme that they name: `routes`: each token names two different experts; in each aligned block of 64 tokens no expert is named by more than 20 tokens, and some blocks reach exactly 20.
All inputs are finite; a program needn't handle non-finite values.
Results may differ from the reference program's by a relative error of at most 0.0071.
Values may be sent and summed in bfloat16 or wider, within the bound.
A program may use at most 128 MiB of HBM per device.

```python
import math
import jax
import jax.numpy as jnp
import numpy as np
from jax import lax

QUERY_GROUP_COUNT = 48
HEAD_DIM = 128
D = 6144
FF = 9216
EXPERTS = 8
TOK_BLK = 64
CAP = 20
PROMPT_LENGTH = 4096
SLOTS = 1280
N_SEQ = 64


def draw_log_decay(key, part):
    generator_children = jax.random.split(key, 5)
    picker = jax.random.uniform(generator_children[0], (QUERY_GROUP_COUNT, 1))
    level = jax.random.uniform(generator_children[1], (QUERY_GROUP_COUNT, 1))
    slow_rate = jnp.exp(jnp.log(1.0 / (4.0 * PROMPT_LENGTH)) + level * jnp.log(4.0))
    fast_rate = jnp.exp(jnp.log(1.0 / PROMPT_LENGTH) + level * jnp.log(PROMPT_LENGTH / 30.0))
    forgetting_factor = jnp.where(picker < 0.5, slow_rate, fast_rate)
    stochastic_perturbation = jnp.exp(jax.random.uniform(generator_children[2], (QUERY_GROUP_COUNT, PROMPT_LENGTH), minval=jnp.log(0.5), maxval=jnp.log(2.0)))
    spike_occurrences = jax.random.uniform(generator_children[3], (QUERY_GROUP_COUNT, PROMPT_LENGTH)) < 3.0 / PROMPT_LENGTH
    objective_samples = jnp.log(jax.random.uniform(generator_children[4], (QUERY_GROUP_COUNT, PROMPT_LENGTH), minval=0.5, maxval=0.8))
    return (-forgetting_factor * stochastic_perturbation + jnp.where(spike_occurrences, objective_samples, 0.0)).astype(jnp.float32)


def level_of(own_key, extent, pieces, least, high):
    def one(axis_at, shards_of):
        heights = jax.random.uniform(jax.random.fold_in(jax.random.fold_in(own_key, 6), axis_at), (shards_of,), jnp.float32, least / len(pieces), high / len(pieces))
        return jnp.repeat(jnp.exp(heights), extent[axis_at] // shards_of).reshape((-1,) + (1,) * (len(extent) - axis_at - 1))

    factor_of = one(*pieces[0])
    for cut in pieces[1:]:
        factor_of = factor_of * one(*cut)
    return factor_of


def assign_block(key, own, number, rows, number_of, top, limit, slope):
    ranking = jax.random.permutation(key, number_of)
    crowded, ordinary = shares(number_of, rows * top, limit, slope, True), shares(number_of, rows * top, limit, slope, False)
    places = jnp.arange(number_of)

    def named(sizes, turn):
        used = int((sizes > 0).sum())
        fixed = max(1, used // 4)
        moved = fixed + (places - fixed + turn * (used - fixed)) % max(1, number_of - fixed)
        return jnp.zeros((number_of,), jnp.int32).at[ranking[jnp.where(places < fixed, places, moved)]].set(jnp.asarray(sizes, jnp.int32))

    sizes = jnp.where(number % 4 == 0, named(crowded, number // 4), named(ordinary, number - number // 4 - 1))
    mixed = jax.random.permutation(jax.random.fold_in(own, 3), number_of)
    giver, sink = mixed[0:number_of // 2 * 2:2], mixed[1:number_of // 2 * 2:2]
    room = jnp.minimum(sizes[giver] - 1, limit - sizes[sink]) // 2
    room = jnp.where((giver == ranking[0]) | (sink == ranking[0]) | (sizes[sink] == 0), 0, jnp.maximum(room, 0))
    moved = jax.random.randint(jax.random.fold_in(own, 4), (number_of // 2,), 0, 1 << 20) % (room + 1)
    sizes = sizes.at[giver].add(-moved).at[sink].add(moved)
    items = jnp.searchsorted(jnp.cumsum(sizes), jnp.arange(rows * top), side="right").astype(jnp.int32)
    listing = items.reshape(top, rows).T
    listing = listing[jax.random.permutation(jax.random.fold_in(own, 1), rows)]
    turn = jax.random.randint(jax.random.fold_in(own, 2), (rows, 1), 0, top)
    return jnp.take_along_axis(listing, (jnp.arange(top)[None, :] + turn) % top, axis=1)


def shares(count, total, reach, slope, full):
    loads = [(1 << 20) // math.isqrt(rank ** slope) + 1 for rank in range(1, count + 1)]
    largest = reach if full else min(reach, max(-(-total // count), total * loads[0] // sum(loads)))
    least = 1 if total - largest >= count - 1 else 0
    counts, surplus = [largest] + [least] * (count - 1), total - largest - least * (count - 1)
    while surplus > 0:
        movable = [i for i in range(1, count) if counts[i] < largest] or [i for i in range(1, count) if counts[i] < reach]
        pool, budget = sum([loads[i] for i in movable]), surplus
        for i in movable:
            more = min(reach - counts[i], max(1, budget * loads[i] // pool), surplus)
            counts[i] = counts[i] + more
            surplus = surplus - more
    return np.array(counts)


def scatter_about(rng, shape, width, limit, cuts=(), kind=jnp.bfloat16):
    loudness = level_of(rng, shape, cuts, -0.22, 0.18) if cuts else 1.0
    values = jax.random.normal(rng, shape, jnp.float32) * width * loudness
    return jnp.minimum(jnp.maximum(values, -limit), limit).astype(kind)


def setup_inputs(seed: int = 0) -> dict:
    key_of = jax.random.split(jax.random.key(seed), 10)
    queries = scatter_about(key_of[0], (PROMPT_LENGTH, D), 1.0, 6.0, ((0, 64), (1, 8)))
    keys = scatter_about(key_of[1], (PROMPT_LENGTH, D), 1.0, 6.0, ((0, 64), (1, 8)))
    values = scatter_about(key_of[2], (PROMPT_LENGTH, D), 1.0, 6.0, ((0, 64), (1, 8)))
    log_decay = draw_log_decay(jax.random.fold_in(key_of[9], 71), 0)
    state_in = scatter_about(key_of[4], (QUERY_GROUP_COUNT, HEAD_DIM, HEAD_DIM), 4.0, 24.0, ((0, 8),), jnp.float32)
    norm_gain = jnp.clip(1.0 + 0.18 * jax.random.normal(key_of[5], (D,), jnp.float32), 0.1, 1.9)
    routes_keys = jax.random.split(jax.random.fold_in(key_of[6], 1), PROMPT_LENGTH // TOK_BLK)
    routes_turns = jax.random.permutation(jax.random.fold_in(key_of[6], 3), PROMPT_LENGTH // TOK_BLK)
    routes = jax.vmap(lambda own, number: assign_block(jax.random.fold_in(key_of[6], 2), own, number, TOK_BLK, EXPERTS, 2, CAP, 2))(routes_keys, routes_turns).reshape((PROMPT_LENGTH, 2))
    w_gate = scatter_about(key_of[7], (EXPERTS, FF, D), D ** -0.5, 0.078125, ((0, 8), (1, 64)))
    w_up = scatter_about(key_of[8], (EXPERTS, FF, D), D ** -0.5, 0.078125, ((0, 8), (1, 64)))
    return {"queries": queries, "keys": keys, "values": values, "log_decay": log_decay, "state_in": state_in, "norm_gain": norm_gain, "routes": routes, "w_gate": w_gate, "w_up": w_up}


epsilon = 1e-06

def reference(queries, keys, values, log_decay, state_in, norm_gain, routes, w_gate, w_up):
    heads = state_in.shape[0]
    head_dim = state_in.shape[1]
    scaling = 1.0 / math.sqrt(head_dim)
    query_all = queries.reshape(N_SEQ, TOK_BLK, heads, head_dim)
    key_all = keys.reshape(N_SEQ, TOK_BLK, heads, head_dim)
    value_all = values.reshape(N_SEQ, TOK_BLK, heads, head_dim)
    log_blocks = log_decay.reshape(heads, N_SEQ, TOK_BLK).transpose(1, 0, 2)
    causal = jnp.arange(TOK_BLK)[:, None] >= jnp.arange(TOK_BLK)[None, :]

    def block_step(running, inputs):
        query_blk, key_blk, value_blk, log_blk = inputs
        cumlog = jnp.cumsum(log_blk, axis=1)
        block_log = cumlog[:, -1]
        scores = jnp.einsum('ihd,jhd->hij', query_blk.astype(jnp.float32), key_blk.astype(jnp.float32), precision=lax.Precision.HIGHEST) * scaling
        gap_log = cumlog[:, :, None] - cumlog[:, None, :]
        weights = jnp.where(causal[None], jnp.exp(jnp.where(causal[None], gap_log, 0.0)), 0.0)
        decayed = (scores * weights).astype(jnp.bfloat16)
        inside = jnp.einsum('hij,jhd->ihd', decayed.astype(jnp.float32), value_blk.astype(jnp.float32), precision=lax.Precision.HIGHEST)
        key_weighted = key_blk.astype(jnp.float32) * jnp.exp(block_log[:, None] - cumlog).T[:, :, None]
        block_state = jnp.einsum('jhd,jhe->hde', key_weighted, value_blk.astype(jnp.float32), precision=lax.Precision.HIGHEST)
        carried_in = jnp.einsum('ihd,hde->ihe', query_blk.astype(jnp.float32) * scaling, running, precision=lax.Precision.HIGHEST)
        carried_in = carried_in * jnp.exp(cumlog).T[:, :, None]
        updated = jnp.exp(block_log)[:, None, None] * running + block_state
        return (updated, inside + carried_in)
    final_state, block_outs = lax.scan(block_step, state_in, (query_all, key_all, value_all, log_blocks))
    attended = block_outs.reshape(PROMPT_LENGTH, heads * head_dim).astype(jnp.bfloat16)
    att_wide = attended.astype(jnp.float32)
    normed = (att_wide * lax.rsqrt(lax.optimization_barrier(jnp.mean(att_wide * att_wide, axis=1, keepdims=True)) + epsilon) * norm_gain).astype(jnp.bfloat16)
    blocks = jnp.arange(PROMPT_LENGTH, dtype=jnp.int32) // TOK_BLK

    def one_expert(expert_id):
        chosen = jnp.any(routes == expert_id, axis=1).astype(jnp.int32)
        position = jnp.cumsum(chosen.reshape(N_SEQ, TOK_BLK), axis=1).reshape(PROMPT_LENGTH).astype(jnp.int32) - 1
        slot_ids = jnp.where(chosen == 1, blocks * CAP + position, SLOTS).astype(jnp.int32)
        row_set = jnp.zeros((SLOTS, D), normed.dtype).at[slot_ids].set(normed, mode='drop')
        gate_act = jnp.dot(w_gate[expert_id], row_set.T, preferred_element_type=jnp.float32)
        up_act = jnp.dot(w_up[expert_id], row_set.T, preferred_element_type=jnp.float32)
        return (jax.nn.silu(gate_act) * up_act).astype(jnp.bfloat16)
    expert_hidden = lax.map(one_expert, jnp.arange(EXPERTS, dtype=jnp.int32))
    return (expert_hidden, final_state)
```

```python
import functools
import math

import jax
import jax.numpy as jnp
from jax import lax
from jax.experimental import pallas as pl
from jax.experimental.pallas import tpu as pltpu
from jax.sharding import PartitionSpec as P

MESH = pl.DeviceIdType.MESH
CAP = 20
EPSILON = 1e-06
NX = 4
HIGHEST = lax.Precision.HIGHEST
F32, BF16 = jnp.float32, jnp.bfloat16


def iota(shape, dim):
    return lax.broadcasted_iota(jnp.int32, shape, dim)


def dot(a, b, dims=((1,), (0,)), precision=None):
    return lax.dot_general(a, b, (dims, ((), ())), precision=precision, preferred_element_type=F32)


def remote(src, dst, send, recv, where):
    return pltpu.make_async_remote_copy(
        src_ref=src, dst_ref=dst, send_sem=send, recv_sem=recv, device_id=where, device_id_type=MESH
    )


def enter(peers):
    barrier = pltpu.get_barrier_semaphore()
    for peer in peers:
        pl.semaphore_signal(barrier, inc=1, device_id=peer, device_id_type=MESH)
    pl.semaphore_wait(barrier, len(peers))


def attend_kernel(
    nz, ne, q_ref, k_ref, v_ref, ld_ref, sin_ref, routes_ref, gain_ref, gain4_ref,
    unit_ref, sout_ref,
    stage, send1, recv1, xbuf, send2, recv2, ent, att, sende, recve,
    s1, r1, sx_sem, rx_sem, s2, r2, se, re,
):
    tokens = q_ref.shape[0]
    heads = ld_ref.shape[0]
    hd = sin_ref.shape[1]
    rows = hd // nz
    part = rows // NX
    width = heads * hd
    scaling = 1.0 / math.sqrt(hd)
    place = lax.axis_index("seq")
    x, z = place // nz, place % nz
    me = lax.axis_index("exp")
    zpeers = [(j, lax.rem(z + j, nz)) for j in range(1, nz)]
    xpeers = [(j, lax.rem(x + j, NX)) for j in range(1, NX)]
    epeers = [(j, lax.rem(me + j, ne)) for j in range(1, ne)]
    enter(
        [{"seq": x * nz + p} for _, p in zpeers]
        + [{"seq": p * nz + z} for _, p in xpeers]
        + [{"exp": p} for _, p in epeers]
    )

    ld = ld_ref[...]
    at_or_before = (iota((tokens, tokens), 0) <= iota((tokens, tokens), 1)).astype(F32)
    causal = iota((tokens, tokens), 0) >= iota((tokens, tokens), 1)
    cum = dot(ld, at_or_before, precision=HIGHEST)
    cumt = dot(causal.astype(F32), ld, ((1,), (1,)), HIGHEST)

    d = iota((hd, hd), 0)
    per_x = hd // NX
    order = (d % per_x) // part * rows + d // per_x * part + d % part
    perm = (order == iota((hd, hd), 1)).astype(BF16)

    def cols(h):
        return slice(h * hd, (h + 1) * hd)

    qs, ks = [], []
    for h in range(heads):
        qs.append(dot(q_ref[:, cols(h)], perm).astype(BF16))
        ks.append(dot(k_ref[:, cols(h)], perm).astype(BF16))
    for h in range(heads):
        last = cum[h : h + 1, tokens - 1 : tokens]
        kw = ks[h].astype(F32) * jnp.exp(last - cumt[:, h : h + 1])
        high = kw.astype(BF16)
        low = (kw - high.astype(F32)).astype(BF16)
        vh = v_ref[:, cols(h)]
        state = dot(high, vh, ((0,), (0,))) + dot(low, vh, ((0,), (0,)))
        stage[:, h * rows : (h + 1) * rows, :] = state.reshape(nz, rows, hd)
    srows = heads * rows
    send1[:, 0:srows, :] = stage[...].astype(BF16)
    total = jnp.broadcast_to(cum[:, tokens - 1 : tokens], (heads, hd))
    total = jnp.concatenate([total, jnp.zeros((8 - heads, hd), F32)], axis=0)
    high = total.astype(BF16).astype(F32)
    logs = jnp.concatenate([high, total - high], axis=0).astype(BF16)
    send1[:, srows : srows + 16, :] = jnp.broadcast_to(logs[None], (nz, 16, hd))

    firsts = []
    for j, p in zpeers:
        c = remote(send1.at[p], recv1.at[z], s1.at[j], r1.at[j], {"seq": x * nz + p})
        c.start()
        firsts.append(c)
    recv1[z] = send1[z]

    for h in range(heads):
        scores = dot(qs[h], ks[h], ((1,), (1,))) * scaling
        gap = cumt[:, h : h + 1] - cum[h : h + 1, :]
        weights = jnp.where(causal, jnp.exp(jnp.where(causal, gap, 0.0)), 0.0)
        att[:, cols(h)] = dot((scores * weights).astype(BF16), v_ref[:, cols(h)])

    group = me // (ne // 4)
    expert = iota((ne, tokens), 0)
    chosen = (routes_ref[0:1, :] == expert) | (routes_ref[1:2, :] == expert)
    position = dot(chosen.astype(F32), at_or_before, precision=HIGHEST) - 1.0
    position = jnp.where(chosen, position, -1.0)
    line = iota((32, tokens), 0)
    slot = jnp.where(line < 16, line, jnp.where((line - 16) // 4 == group, 16 + line % 4, -5))
    slot = slot.astype(F32)
    selector = jnp.concatenate(
        [
            (jnp.abs(slot - position[e : e + 1, :]) < 0.5).astype(F32).astype(BF16)
            for e in range(ne)
        ],
        axis=0,
    )

    for j, p in zpeers:
        src = lax.rem(z + nz - j, nz)
        remote(send1.at[src], recv1.at[src], s1.at[j], r1.at[j], {"seq": x * nz + src}).wait_recv()

    def block(j):
        piece = recv1[j].astype(F32)
        logs = piece[srows : srows + 8] + piece[srows + 8 : srows + 16]
        return piece, logs

    def step(running, piece, decay):
        return [
            decay[h : h + 1, :] * running[h] + piece[h * rows : (h + 1) * rows]
            for h in range(heads)
        ]

    running = [jnp.zeros((rows, hd), F32)] * heads
    whole = jnp.zeros((8, hd), F32)
    for j in range(nz):
        piece, logs = block(j)
        running = step(running, piece, jnp.exp(logs))
        whole = whole + logs
    for h in range(heads):
        xbuf[x, h * rows : (h + 1) * rows, :] = running[h]
    xbuf[x, srows : srows + 8, :] = whole
    seconds = []
    for j, p in xpeers:
        c = remote(xbuf.at[x], xbuf.at[x], sx_sem.at[j], rx_sem.at[j], {"seq": p * nz + z})
        c.start()
        seconds.append(c)
    for j, p in xpeers:
        src = lax.rem(x + NX - j, NX)
        remote(
            xbuf.at[src], xbuf.at[src], sx_sem.at[j], rx_sem.at[j], {"seq": src * nz + z}
        ).wait_recv()

    final = [sin_ref[h * rows : (h + 1) * rows, :] for h in range(heads)]
    entering = final
    for g in range(NX):
        entering = [jnp.where(x == g, f, e) for f, e in zip(final, entering)]
        final = step(final, xbuf[g], jnp.exp(xbuf[g, srows : srows + 8, :]))
    for j in range(nz):
        send2[j] = jnp.concatenate(entering, axis=0).astype(BF16)
        if j < nz - 1:
            piece, logs = block(j)
            entering = step(entering, piece, jnp.exp(logs))
    thirds = []
    for j, p in zpeers:
        c = remote(send2.at[p], recv2.at[z], s2.at[j], r2.at[j], {"seq": x * nz + p})
        c.start()
        thirds.append(c)
    recv2[z] = send2[z]
    for h in range(heads):
        mine = jnp.zeros((part, hd), F32)
        for g in range(NX):
            mine = jnp.where(x == g, final[h][g * part : (g + 1) * part], mine)
        sout_ref[h] = mine
    for j, p in zpeers:
        src = lax.rem(z + nz - j, nz)
        remote(send2.at[src], recv2.at[src], s2.at[j], r2.at[j], {"seq": x * nz + src}).wait_recv()

    ent[...] = recv2[...].astype(F32)
    parts = []
    for h in range(heads):
        state = ent[:, h * rows : (h + 1) * rows, :].reshape(hd, hd).astype(BF16)
        carried = dot(qs[h], state) * scaling * jnp.exp(cumt[:, h : h + 1])
        parts.append((att[:, cols(h)] + carried).astype(BF16))
    attended = jnp.concatenate(parts, axis=1)
    for e in range(ne):
        sende[e] = dot(selector[e * 32 : (e + 1) * 32], attended).astype(BF16)
    fourths = []
    for j, p in epeers:
        c = remote(sende.at[p], recve.at[me], se.at[j], re.at[j], {"exp": p})
        c.start()
        fourths.append(c)
    recve[me] = sende[me]
    for j, p in epeers:
        src = lax.rem(me + ne - j, ne)
        remote(sende.at[src], recve.at[src], se.at[j], re.at[j], {"exp": src}).wait_recv()

    depth = ne * width
    wide = [recve[e].astype(F32) for e in range(ne)]
    main = [w[0:16] for w in wide]
    halves = ne // 4
    rest = [sum(wide[g * halves + i][16:32] for g in range(4)) for i in range(halves)]
    square = sum(jnp.sum(m * m, axis=1, keepdims=True) for m in main)
    scale = lax.rsqrt(square / depth + EPSILON)
    for e in range(ne):
        at = slice(e * width, (e + 1) * width)
        unit_ref[:, at] = (main[e] * scale * gain_ref[:, at]).astype(BF16)
    square = sum(jnp.sum(m * m, axis=1, keepdims=True) for m in rest)
    same = (iota((16, 16), 0) % 4 == iota((16, 16), 1) % 4).astype(F32)
    square = dot(same, jnp.broadcast_to(square, (16, 128)), precision=HIGHEST)[:, 0:1]
    scale = lax.rsqrt(square / depth + EPSILON)
    for i in range(halves):
        at = slice(i * width, (i + 1) * width)
        unit_ref[:, depth + i * width : depth + (i + 1) * width] = (
            rest[i] * scale * gain4_ref[:, at]
        ).astype(BF16)

    for c in firsts + seconds + thirds + fourths:
        c.wait_send()


def attend(nz, ne, q, k, v, ld, sin, routes, gain, gain4):
    tokens, width = q.shape
    heads, hd = ld.shape[0], sin.shape[1]
    rows = hd // nz
    depth = ne * width
    dma = pltpu.SemaphoreType.DMA
    vmem = pl.BlockSpec(memory_space=pltpu.VMEM)
    return pl.pallas_call(
        functools.partial(attend_kernel, nz, ne),
        out_shape=(
            jax.ShapeDtypeStruct((16, depth + depth // 4), BF16),
            jax.ShapeDtypeStruct((heads, rows // NX, hd), F32),
        ),
        in_specs=[vmem] * 8,
        out_specs=(vmem, vmem),
        scratch_shapes=[
            pltpu.VMEM((nz, heads * rows, hd), F32),
            pltpu.VMEM((nz, heads * rows + 16, hd), BF16),
            pltpu.VMEM((nz, heads * rows + 16, hd), BF16),
            pltpu.VMEM((NX, heads * rows + 8, hd), F32),
            pltpu.VMEM((nz, heads * rows, hd), BF16),
            pltpu.VMEM((nz, heads * rows, hd), BF16),
            pltpu.VMEM((nz, heads * rows, hd), F32),
            pltpu.VMEM((tokens, width), F32),
            pltpu.VMEM((ne, 32, width), BF16),
            pltpu.VMEM((ne, 32, width), BF16),
            dma((nz,)),
            dma((nz,)),
            dma((NX,)),
            dma((NX,)),
            dma((nz,)),
            dma((nz,)),
            dma((ne,)),
            dma((ne,)),
        ],
        compiler_params=pltpu.CompilerParams(
            collective_id=0, has_side_effects=True, vmem_limit_bytes=48 * 2**20
        ),
    )(q, k, v, ld, sin, routes, gain, gain4)


def experts_kernel(
    nz, unit_ref, gate_ref, up_ref, out_ref,
    bufa, bufb, wbuf, acc, own_sem, sa1, ra1, sa2, ra2, sb1, rb1, sb2, rb2,
):
    hidden = gate_ref.shape[1]
    depth = gate_ref.shape[2]
    quarter = depth // 4
    ka = bufa.shape[2]
    long, short = nz // 2, nz - 1 - nz // 2
    place = lax.axis_index("seq")
    x, z = place // nz, place % nz
    core = lax.axis_index("exp") % 2
    d = 1 - 2 * core

    def zat(k):
        return lax.rem(z + k * d + 2 * nz, nz)

    def xat(k):
        return lax.rem(x + k * d + 2 * NX, NX)

    loads = [
        pltpu.make_async_copy(unit_ref.at[:, pl.ds(0, ka)], bufa.at[z * NX + x], own_sem.at[0]),
        pltpu.make_async_copy(
            unit_ref.at[:, pl.ds(ka, unit_ref.shape[1] - ka)], bufb.at[z * NX + x], own_sem.at[1]
        ),
        pltpu.make_async_copy(gate_ref.at[0], wbuf.at[pl.ds(0, hidden)], own_sem.at[2]),
        pltpu.make_async_copy(up_ref.at[0], wbuf.at[pl.ds(hidden, hidden)], own_sem.at[3]),
    ]
    for c in loads:
        c.start()
    to_z = [{"seq": x * nz + zat(1)}, {"seq": x * nz + zat(-1)}]
    to_x = [{"seq": xat(j) * nz + z} for j in range(NX)]
    enter(to_z + to_x[1:])
    loads[0].wait()
    loads[1].wait()

    def a1(j):
        return remote(
            bufa.at[z * NX + x], bufa.at[z * NX + x], sa1.at[0], ra1.at[j - 1], to_x[j]
        )

    def a1_arrived(j):
        u = z * NX + xat(-j)
        return remote(bufa.at[u], bufa.at[u], sa1.at[0], ra1.at[j - 1], to_x[j])

    def a2(way, k, c):
        u = zat(-k if way == 0 else k) * NX + xat(-c)
        return remote(bufa.at[u], bufa.at[u], sa2.at[way], ra2.at[way, k, c], to_z[way])

    def a2_arrived(way, k, c):
        u = zat(-k - 1 if way == 0 else k + 1) * NX + xat(-c)
        return remote(bufa.at[u], bufa.at[u], sa2.at[way], ra2.at[way, k, c], to_z[way])

    def b1(way, k):
        u = zat(-k if way == 0 else k) * NX + x
        return remote(bufb.at[u], bufb.at[u], sb1.at[way], rb1.at[way, k], to_z[way])

    def b1_arrived(way, k):
        u = zat(-k - 1 if way == 0 else k + 1) * NX + x
        return remote(bufb.at[u], bufb.at[u], sb1.at[way], rb1.at[way, k], to_z[way])

    def b2(o, kind):
        u = zat(o) * NX + (x if kind < 2 else xat(-1))
        where = to_x[NX - 1] if kind == 1 else to_x[1]
        return remote(bufb.at[u], bufb.at[u], sb2.at[0], rb2.at[kind, o + nz], where)

    def b2_arrived(o, kind):
        u = zat(o) * NX + xat((-1, 1, -2)[kind])
        where = to_x[NX - 1] if kind == 1 else to_x[1]
        return remote(bufb.at[u], bufb.at[u], sb2.at[0], rb2.at[kind, o + nz], where)

    def spread(o):
        b2(o, 0).start()
        b2(o, 1).start()

    def forward(o):
        b2_arrived(o, 0).wait_recv()
        b2(o, 2).start()

    def finish(o):
        b2_arrived(o, 1).wait_recv()
        b2_arrived(o, 2).wait_recv()

    lanes = 16 * NX

    def compute(offsets):
        n = lanes * len(offsets)
        zs = [zat(o) for o in offsets]

        def stacked(buf, start, size):
            got = [
                buf[pl.ds(zz * NX, NX), :, start : start + size].reshape(lanes, size) for zz in zs
            ]
            return got[0] if len(got) == 1 else jnp.concatenate(got, axis=0)

        t = ((1,), (1,))
        main = dot(wbuf[:, 0:ka], stacked(bufa, 0, ka), t)
        main = main + dot(wbuf[:, ka:depth], stacked(bufb, 0, depth - ka), t)
        tail = stacked(bufb, depth - ka, quarter)
        lane = iota((2 * hidden, n), 1)
        rest = jnp.zeros((2 * hidden, n), F32)
        for g in range(4):
            one = dot(wbuf[:, g * quarter : (g + 1) * quarter], tail, t)
            rest = rest + jnp.where(lane % 16 // 4 == g, one, 0.0)
        if n < 128:
            rest = jnp.concatenate([rest, jnp.zeros((2 * hidden, 128 - n), F32)], axis=1)
            main = jnp.concatenate([main, jnp.zeros((2 * hidden, 128 - n), F32)], axis=1)
        rest = sum([pltpu.roll(rest, 4 * g, 1) for g in range(1, 4)], rest)

        def gated(a):
            gate, up = a[0:hidden], a[hidden : 2 * hidden]
            return (gate / (1.0 + jnp.exp(-gate)) * up).astype(BF16)

        columns = acc.shape[1]
        l = iota((128, columns), 0)
        r = l % 16
        start = zs[0] * CAP if len(zs) == 1 else jnp.where(l < lanes, zs[0], zs[1]) * CAP
        start = start + l % lanes // 16 * (nz * CAP)
        n_at = iota((128, columns), 1)
        used = l < n
        p_main = ((n_at == start + r) & used).astype(F32).astype(BF16)
        p_rest = ((n_at == start + 16 + r % 4) & (r >= 12) & used).astype(F32).astype(BF16)
        acc[...] += dot(gated(main), p_main) + dot(gated(rest), p_rest)

    acc[...] = jnp.zeros_like(acc)

    spread(0)
    for j in (1, 3, 2):
        a1(j).start()
    for way in range(2):
        b1(way, 0).start()
        a2(way, 0, 0).start()
    for c in (1, 3, 2):
        a1_arrived(c).wait_recv()
        for way in range(2):
            a2(way, 0, c).start()
    for way, o in ((0, -1), (1, 1)):
        b1_arrived(way, 0).wait_recv()
        b1(way, 1).start()
        spread(o)
    loads[2].wait()
    loads[3].wait()
    forward(0)

    def turn(t, first):
        for c in (0, 1):
            for way in range(2):
                a2_arrived(way, t - 1, c).wait_recv()
                a2(way, t, c).start()
        for way in range(2):
            b1_arrived(way, t).wait_recv()
            b1(way, t + 1).start()
            spread(-t - 1 if way == 0 else t + 1)
        for c in (3, 2):
            for way in range(2):
                a2_arrived(way, t - 1, c).wait_recv()
                a2(way, t, c).start()
        forward(-t)
        forward(t)
        if first:
            finish(0)
            compute([0])
        else:
            finish(1 - t)
            finish(t - 1)
            compute([1 - t, t - 1])

    turn(1, True)

    @pl.loop(2, short - 1)
    def _(t):
        turn(t, False)

    t = short - 1
    for c in (0, 1, 3, 2):
        for way in range(2):
            a2_arrived(way, t - 1, c).wait_recv()
            a2(way, t, c).start()
        if c == 1:
            b1_arrived(0, t).wait_recv()
            b1(0, t + 1).start()
            spread(-t - 1)
            b1_arrived(1, t).wait_recv()
            spread(t + 1)
    forward(-t)
    forward(t)
    finish(1 - t)
    finish(t - 1)
    compute([1 - t, t - 1])
    t = long - 1
    for c in (0, 1, 3, 2):
        a2_arrived(0, t - 1, c).wait_recv()
        a2(0, t, c).start()
        a2_arrived(1, t - 1, c).wait_recv()
        if c == 1:
            b1_arrived(0, t).wait_recv()
            spread(-t - 1)
    forward(-t)
    forward(t)
    finish(1 - t)
    finish(t - 1)
    compute([1 - t, t - 1])
    forward(-long)
    finish(-t)
    finish(t)
    compute([-t, t])
    for c in (0, 1, 3, 2):
        a2_arrived(0, t, c).wait_recv()
    finish(-long)
    compute([-long])
    out_ref[0] = acc[...].astype(BF16)

    def sent(buf, count, sem):
        span = buf.at[pl.ds(0, count)]
        remote(span, span, sem, ra1.at[0], to_z[0]).wait_send()

    sent(bufa, NX - 1, sa1.at[0])
    sent(bufa, NX * long, sa2.at[0])
    sent(bufa, NX * short, sa2.at[1])
    sent(bufb, long, sb1.at[0])
    sent(bufb, short, sb1.at[1])
    sent(bufb, 3 * nz, sb2.at[0])


def experts(nz, unit, w_gate, w_up):
    _, hidden, depth = w_gate.shape
    ka = depth * 22 // 48 // 128 * 128
    kb = unit.shape[1] - ka
    units = NX * nz
    long = nz // 2
    dma = pltpu.SemaphoreType.DMA
    anywhere = pl.BlockSpec(memory_space=pl.ANY)
    return pl.pallas_call(
        functools.partial(experts_kernel, nz),
        out_shape=jax.ShapeDtypeStruct((1, hidden, units * CAP), BF16),
        in_specs=[anywhere] * 3,
        out_specs=pl.BlockSpec(memory_space=pltpu.VMEM),
        scratch_shapes=[
            pltpu.VMEM((units, 16, ka), BF16),
            pltpu.VMEM((units, 16, kb), BF16),
            pltpu.VMEM((2 * hidden, depth), BF16),
            pltpu.VMEM((hidden, units * CAP), F32),
            dma((4,)),
            dma((1,)),
            dma((NX - 1,)),
            dma((2,)),
            dma((2, long, NX)),
            dma((2,)),
            dma((2, long)),
            dma((1,)),
            dma((3, 2 * nz)),
        ],
        compiler_params=pltpu.CompilerParams(
            collective_id=1, has_side_effects=True, vmem_limit_bytes=48 * 2**20
        ),
    )(unit, w_gate, w_up)


def shards(nz, ne, queries, keys, values, log_decay, state_in, norm_gain, routes, w_gate, w_up):
    heads, hd, _ = state_in.shape
    place = lax.axis_index("seq")
    rows = hd // nz
    part = rows // NX
    carried = lax.dynamic_slice_in_dim(
        state_in.reshape(heads, NX, hd // NX, hd), place % nz * part, part, 2
    ).reshape(heads * rows, hd)
    depth = norm_gain.shape[0]
    gain4 = jnp.repeat(norm_gain.reshape(4, depth // 4), 4, axis=0)
    unit, state_out = attend(
        nz, ne, queries, keys, values, log_decay, carried, routes.T, norm_gain[None], gain4
    )
    return experts(nz, unit, w_gate, w_up), state_out


def solution(mesh):
    placed = (
        P("seq", "exp"),
        P("seq", "exp"),
        P("seq", "exp"),
        P("exp", "seq"),
        P("exp", None, None),
        P(),
        P("seq", None),
        P("exp", "seq", None),
        P("exp", "seq", None),
    )
    return jax.shard_map(
        functools.partial(shards, mesh.shape["seq"] // NX, mesh.shape["exp"]),
        mesh=mesh,
        in_specs=placed,
        out_specs=(P("exp", "seq", None), P("exp", "seq", None)),
        check_vma=False,
    )
```

```python
import functools
import math

import jax
import jax.numpy as jnp
from jax import lax
from jax.experimental import pallas as pl
from jax.experimental.pallas import tpu as pltpu
from jax.sharding import PartitionSpec as P

MESH = pl.DeviceIdType.MESH
CAP = 20
EPSILON = 1e-06
NX = 4
HIGHEST = lax.Precision.HIGHEST
F32, BF16 = jnp.float32, jnp.bfloat16


def iota(shape, dim):
    return lax.broadcasted_iota(jnp.int32, shape, dim)


def dot(a, b, dims=((1,), (0,)), precision=None):
    return lax.dot_general(a, b, (dims, ((), ())), precision=precision, preferred_element_type=F32)


def remote(src, dst, send, recv, where):
    return pltpu.make_async_remote_copy(
        src_ref=src, dst_ref=dst, send_sem=send, recv_sem=recv, device_id=where, device_id_type=MESH
    )


def enter(peers):
    barrier = pltpu.get_barrier_semaphore()
    for peer in peers:
        pl.semaphore_signal(barrier, inc=1, device_id=peer, device_id_type=MESH)
    pl.semaphore_wait(barrier, len(peers))


def block_kernel(
    nz, ne, q_hbm, k_hbm, v_hbm, ld_hbm, sin_hbm, routes_hbm, gain_hbm, gate_hbm, up_hbm,
    out_ref, sout_ref,
    q_ref, k_ref, v_ref, ld_ref, sin_ref, routes_ref, gain_ref, wbuf,
    stage, send1, recv1, logs, xbuf, send2, recv2, ent, att, sende, recve,
    bufa, bufb, acc,
    load, sl, rl, s1, r1, sx_sem, rx_sem, s2, r2, se, re,
    sa1, ra1, sa2, ra2, sb1, rb1, sb2, rb2,
):
    hidden = gate_hbm.shape[1]
    pairs = [
        (q_hbm, q_ref), (k_hbm, k_ref), (v_hbm, v_ref), (ld_hbm, ld_ref), (sin_hbm, sin_ref),
        (routes_hbm, routes_ref), (gain_hbm, gain_ref),
        (gate_hbm.at[0], wbuf.at[pl.ds(0, hidden)]), (up_hbm.at[0], wbuf.at[pl.ds(hidden, hidden)]),
    ]
    loads = [pltpu.make_async_copy(a, b, load.at[i]) for i, (a, b) in enumerate(pairs)]
    for c in loads:
        c.start()

    tokens = q_ref.shape[0]
    heads = ld_ref.shape[0]
    hd = sin_ref.shape[1]
    rows = hd // nz
    part = rows // NX
    width = heads * hd
    scaling = 1.0 / math.sqrt(hd)
    place = lax.axis_index("seq")
    x, z = place // nz, place % nz
    me = lax.axis_index("exp")
    far = sorted(range(1, nz), key=lambda j: -min(j, nz - j))
    zpeers = [(j, lax.rem(z + j, nz)) for j in far]
    xpeers = [(j, lax.rem(x + j, NX)) for j in range(1, NX)]
    epeers = [(j, lax.rem(me + j, ne)) for j in range(1, ne)]
    enter(
        [{"seq": x * nz + p} for _, p in zpeers]
        + [{"seq": p * nz + z} for _, p in xpeers]
        + [{"exp": p} for _, p in epeers]
    )
    for c in loads[:5]:
        c.wait()

    ld = ld_ref[...]
    at_or_before = (iota((tokens, tokens), 0) <= iota((tokens, tokens), 1)).astype(F32)
    causal = iota((tokens, tokens), 0) >= iota((tokens, tokens), 1)
    cum = dot(ld, at_or_before, precision=HIGHEST)
    cumt = dot(causal.astype(F32), ld, ((1,), (1,)), HIGHEST)
    lane = iota((1, hd), 1)
    total = jnp.zeros((1, hd), F32)
    for h in range(heads):
        total = jnp.where(lane == h, cumt[tokens - 1 : tokens, h : h + 1], total)
    logs[z] = total
    pending = []
    for j, p in zpeers:
        c = remote(logs.at[z], logs.at[z], sl.at[j], rl.at[j], {"seq": x * nz + p})
        c.start()
        pending.append(c)

    d = iota((hd, hd), 0)
    per_x = hd // NX
    order = (d % per_x) // part * rows + d // per_x * part + d % part
    perm = (order == iota((hd, hd), 1)).astype(BF16)

    def cols(h):
        return slice(h * hd, (h + 1) * hd)

    qs, ks = [], []
    for h in range(heads):
        ks.append(dot(k_ref[:, cols(h)], perm).astype(BF16))
    for h in range(heads):
        last = cum[h : h + 1, tokens - 1 : tokens]
        kw = ks[h].astype(F32) * jnp.exp(last - cumt[:, h : h + 1])
        high = kw.astype(BF16)
        low = (kw - high.astype(F32)).astype(BF16)
        vh = v_ref[:, cols(h)]
        state = dot(high, vh, ((0,), (0,))) + dot(low, vh, ((0,), (0,)))
        stage[:, h * rows : (h + 1) * rows, :] = state.reshape(nz, rows, hd)
    send1[...] = stage[...].astype(BF16)
    for j, p in zpeers:
        c = remote(send1.at[p], recv1.at[z], s1.at[j], r1.at[j], {"seq": x * nz + p})
        c.start()
        pending.append(c)
    recv1[z] = send1[z]

    for h in range(heads):
        qs.append(dot(q_ref[:, cols(h)], perm).astype(BF16))
        scores = dot(qs[h], ks[h], ((1,), (1,))) * scaling
        gap = cumt[:, h : h + 1] - cum[h : h + 1, :]
        weights = jnp.where(causal, jnp.exp(jnp.where(causal, gap, 0.0)), 0.0)
        att[:, cols(h)] = dot((scores * weights).astype(BF16), v_ref[:, cols(h)])

    pick_r, pick_d = iota((rows, hd), 0), iota((rows, hd), 1)
    pick = (pick_d == pick_r // part * per_x + z * part + pick_r % part).astype(F32)
    first = [dot(pick, sin_ref[h], precision=HIGHEST) for h in range(heads)]

    for c in loads[5:]:
        c.wait()
    group = me // (ne // 4)
    expert = iota((ne, tokens), 0)
    chosen = (routes_ref[0:1, :] == expert) | (routes_ref[1:2, :] == expert)
    position = dot(chosen.astype(F32), at_or_before, precision=HIGHEST) - 1.0
    position = jnp.where(chosen, position, -1.0)
    line = iota((32, tokens), 0)
    slot = jnp.where(line < 16, line, jnp.where((line - 16) // 4 == group, 16 + line % 4, -5))
    slot = slot.astype(F32)
    selector = jnp.concatenate(
        [
            (jnp.abs(slot - position[e : e + 1, :]) < 0.5).astype(F32).astype(BF16)
            for e in range(ne)
        ],
        axis=0,
    )
    acc[...] = jnp.zeros_like(acc)

    for j, p in zpeers:
        src = lax.rem(z + nz - j, nz)
        remote(logs.at[src], logs.at[src], sl.at[j], rl.at[j], {"seq": x * nz + src}).wait_recv()
    decays = [jnp.exp(logs[j]) for j in range(nz)]
    whole = sum([logs[j] for j in range(nz)])
    for j, p in zpeers:
        src = lax.rem(z + nz - j, nz)
        remote(send1.at[src], recv1.at[src], s1.at[j], r1.at[j], {"seq": x * nz + src}).wait_recv()

    def step(running, piece, decay):
        return [
            decay[0:1, h : h + 1] * running[h] + piece[h * rows : (h + 1) * rows]
            for h in range(heads)
        ]

    srows = heads * rows
    running = [jnp.zeros((rows, hd), F32)] * heads
    for j in range(nz):
        running = step(running, recv1[j].astype(F32), decays[j])
    for h in range(heads):
        xbuf[x, h * rows : (h + 1) * rows, :] = running[h]
    xbuf[x, srows : srows + 8, :] = jnp.broadcast_to(whole, (8, hd))
    for j, p in xpeers:
        c = remote(xbuf.at[x], xbuf.at[x], sx_sem.at[j], rx_sem.at[j], {"seq": p * nz + z})
        c.start()
        pending.append(c)
    for j, p in xpeers:
        src = lax.rem(x + NX - j, NX)
        remote(
            xbuf.at[src], xbuf.at[src], sx_sem.at[j], rx_sem.at[j], {"seq": src * nz + z}
        ).wait_recv()

    final = first
    entering = first
    for g in range(NX):
        entering = [jnp.where(x == g, f, e) for f, e in zip(final, entering)]
        final = step(final, xbuf[g], jnp.exp(xbuf[g, srows : srows + 8, :]))
    for j in range(nz):
        send2[j] = jnp.concatenate(entering, axis=0).astype(BF16)

        @pl.when(z != j)
        def _(j=j):
            remote(send2.at[j], recv2.at[z], s2.at[j], r2.at[z], {"seq": x * nz + j}).start()

        if j < nz - 1:
            entering = step(entering, recv1[j].astype(F32), decays[j])
    recv2[z] = send2[z]
    for h in range(heads):
        mine = jnp.zeros((part, hd), F32)
        for g in range(NX):
            mine = jnp.where(x == g, final[h][g * part : (g + 1) * part], mine)
        sout_ref[h] = mine
    for j, p in zpeers:
        remote(send2.at[p], recv2.at[p], s2.at[p], r2.at[p], {"seq": x * nz + p}).wait_recv()

    ent[...] = recv2[...].astype(F32)
    parts = []
    for h in range(heads):
        state = ent[:, h * rows : (h + 1) * rows, :].reshape(hd, hd).astype(BF16)
        carried = dot(qs[h], state) * scaling * jnp.exp(cumt[:, h : h + 1])
        parts.append((att[:, cols(h)] + carried).astype(BF16))
    attended = jnp.concatenate(parts, axis=1)
    for e in range(ne):
        sende[e] = dot(selector[e * 32 : (e + 1) * 32], attended).astype(BF16)
    for j, p in epeers:
        c = remote(sende.at[p], recve.at[me], se.at[j], re.at[j], {"exp": p})
        c.start()
        pending.append(c)
    recve[me] = sende[me]
    for j, p in epeers:
        src = lax.rem(me + ne - j, ne)
        remote(sende.at[src], recve.at[src], se.at[j], re.at[j], {"exp": src}).wait_recv()

    depth = ne * width
    quarter = depth // 4
    ka = bufa.shape[2]
    own = z * NX + x

    def put(start, value):
        cut = min(max(ka - start, 0), value.shape[1])
        if cut > 0:
            bufa[own, :, start : start + cut] = value[:, 0:cut]
        if cut < value.shape[1]:
            bufb[own, :, start + cut - ka : start + value.shape[1] - ka] = value[:, cut:]

    wide = [recve[e].astype(F32) for e in range(ne)]
    main = [w[0:16] for w in wide]
    halves = ne // 4
    rest = [sum([wide[g * halves + i][16:32] for g in range(4)]) for i in range(halves)]
    square = sum([jnp.sum(m * m, axis=1, keepdims=True) for m in main])
    scale = lax.rsqrt(square / depth + EPSILON)
    for e in range(ne):
        at = slice(e * width, (e + 1) * width)
        put(e * width, (main[e] * scale * gain_ref[:, at]).astype(BF16))
    square = sum([jnp.sum(m * m, axis=1, keepdims=True) for m in rest])
    same = (iota((16, 16), 0) % 4 == iota((16, 16), 1) % 4).astype(F32)
    square = dot(same, jnp.broadcast_to(square, (16, 128)), precision=HIGHEST)[:, 0:1]
    scale = lax.rsqrt(square / depth + EPSILON)
    line = iota((16, width), 0) // 4
    for i in range(halves):
        gain = jnp.zeros((16, width), F32)
        for g in range(4):
            at = g * quarter + i * width
            gain = jnp.where(line == g, gain_ref[:, at : at + width], gain)
        put(depth + i * width, (rest[i] * scale * gain).astype(BF16))

    long, short = nz // 2, nz - 1 - nz // 2
    d = 1 - 2 * (me % 2)

    def zat(k):
        return lax.rem(z + k * d + 2 * nz, nz)

    def xat(k):
        return lax.rem(x + k * d + 2 * NX, NX)

    to_z = [{"seq": x * nz + zat(1)}, {"seq": x * nz + zat(-1)}]
    to_x = [{"seq": xat(j) * nz + z} for j in range(NX)]

    def a1(j):
        return remote(
            bufa.at[z * NX + x], bufa.at[z * NX + x], sa1.at[0], ra1.at[j - 1], to_x[j]
        )

    def a1_arrived(j):
        u = z * NX + xat(-j)
        return remote(bufa.at[u], bufa.at[u], sa1.at[0], ra1.at[j - 1], to_x[j])

    def a2(way, k, c):
        u = zat(-k if way == 0 else k) * NX + xat(-c)
        return remote(bufa.at[u], bufa.at[u], sa2.at[way], ra2.at[way, k, c], to_z[way])

    def a2_arrived(way, k, c):
        u = zat(-k - 1 if way == 0 else k + 1) * NX + xat(-c)
        return remote(bufa.at[u], bufa.at[u], sa2.at[way], ra2.at[way, k, c], to_z[way])

    def b1(way, k):
        u = zat(-k if way == 0 else k) * NX + x
        return remote(bufb.at[u], bufb.at[u], sb1.at[way], rb1.at[way, k], to_z[way])

    def b1_arrived(way, k):
        u = zat(-k - 1 if way == 0 else k + 1) * NX + x
        return remote(bufb.at[u], bufb.at[u], sb1.at[way], rb1.at[way, k], to_z[way])

    def b2(o, kind):
        u = zat(o) * NX + (x if kind < 2 else xat(-1))
        where = to_x[NX - 1] if kind == 1 else to_x[1]
        return remote(bufb.at[u], bufb.at[u], sb2.at[0], rb2.at[kind, o + nz], where)

    def b2_arrived(o, kind):
        u = zat(o) * NX + xat((-1, 1, -2)[kind])
        where = to_x[NX - 1] if kind == 1 else to_x[1]
        return remote(bufb.at[u], bufb.at[u], sb2.at[0], rb2.at[kind, o + nz], where)

    def spread(o):
        b2(o, 0).start()
        b2(o, 1).start()

    def forward(o):
        b2_arrived(o, 0).wait_recv()
        b2(o, 2).start()

    def finish(o):
        b2_arrived(o, 1).wait_recv()
        b2_arrived(o, 2).wait_recv()

    lanes = 16 * NX

    def compute(offsets):
        n = lanes * len(offsets)
        zs = [zat(o) for o in offsets]

        def stacked(buf, start, size):
            got = [
                buf[pl.ds(zz * NX, NX), :, start : start + size].reshape(lanes, size) for zz in zs
            ]
            return got[0] if len(got) == 1 else jnp.concatenate(got, axis=0)

        t = ((1,), (1,))
        main = dot(wbuf[:, 0:ka], stacked(bufa, 0, ka), t)
        main = main + dot(wbuf[:, ka:depth], stacked(bufb, 0, depth - ka), t)
        tail = stacked(bufb, depth - ka, quarter)
        lane = iota((2 * hidden, n), 1)
        rest = jnp.zeros((2 * hidden, n), F32)
        for g in range(4):
            one = dot(wbuf[:, g * quarter : (g + 1) * quarter], tail, t)
            rest = rest + jnp.where(lane % 16 // 4 == g, one, 0.0)
        if n < 128:
            rest = jnp.concatenate([rest, jnp.zeros((2 * hidden, 128 - n), F32)], axis=1)
            main = jnp.concatenate([main, jnp.zeros((2 * hidden, 128 - n), F32)], axis=1)
        rest = sum([pltpu.roll(rest, 4 * g, 1) for g in range(1, 4)], rest)

        def gated(a):
            gate, up = a[0:hidden], a[hidden : 2 * hidden]
            return (gate / (1.0 + jnp.exp(-gate)) * up).astype(BF16)

        columns = acc.shape[1]
        l = iota((128, columns), 0)
        r = l % 16
        start = zs[0] * CAP if len(zs) == 1 else jnp.where(l < lanes, zs[0], zs[1]) * CAP
        start = start + l % lanes // 16 * (nz * CAP)
        n_at = iota((128, columns), 1)
        used = l < n
        p_main = ((n_at == start + r) & used).astype(F32).astype(BF16)
        p_rest = ((n_at == start + 16 + r % 4) & (r >= 12) & used).astype(F32).astype(BF16)
        acc[...] += dot(gated(main), p_main) + dot(gated(rest), p_rest)

    spread(0)
    for j in (1, 3, 2):
        a1(j).start()
    for way in range(2):
        b1(way, 0).start()
        a2(way, 0, 0).start()
    for c in (1, 3, 2):
        a1_arrived(c).wait_recv()
        for way in range(2):
            a2(way, 0, c).start()
    for way, o in ((0, -1), (1, 1)):
        b1_arrived(way, 0).wait_recv()
        b1(way, 1).start()
        spread(o)
    forward(0)

    def turn(t, first):
        for c in (0, 1):
            for way in range(2):
                a2_arrived(way, t - 1, c).wait_recv()
                a2(way, t, c).start()
        for way in range(2):
            b1_arrived(way, t).wait_recv()
            b1(way, t + 1).start()
            spread(-t - 1 if way == 0 else t + 1)
        for c in (3, 2):
            for way in range(2):
                a2_arrived(way, t - 1, c).wait_recv()
                a2(way, t, c).start()
        forward(-t)
        forward(t)
        if first:
            finish(0)
            compute([0])
        else:
            finish(1 - t)
            finish(t - 1)
            compute([1 - t, t - 1])

    turn(1, True)

    @pl.loop(2, short - 1)
    def _(t):
        turn(t, False)

    t = short - 1
    for c in (0, 1, 3, 2):
        for way in range(2):
            a2_arrived(way, t - 1, c).wait_recv()
            a2(way, t, c).start()
        if c == 1:
            b1_arrived(0, t).wait_recv()
            b1(0, t + 1).start()
            spread(-t - 1)
            b1_arrived(1, t).wait_recv()
            spread(t + 1)
    forward(-t)
    forward(t)
    finish(1 - t)
    finish(t - 1)
    compute([1 - t, t - 1])
    t = long - 1
    for c in (0, 1, 3, 2):
        a2_arrived(0, t - 1, c).wait_recv()
        a2(0, t, c).start()
        a2_arrived(1, t - 1, c).wait_recv()
        if c == 1:
            b1_arrived(0, t).wait_recv()
            spread(-t - 1)
    forward(-t)
    forward(t)
    finish(1 - t)
    finish(t - 1)
    compute([1 - t, t - 1])
    forward(-long)
    finish(-t)
    finish(t)
    compute([-t, t])
    for c in (0, 1, 3, 2):
        a2_arrived(0, t, c).wait_recv()
    finish(-long)
    compute([-long])
    out_ref[0] = acc[...].astype(BF16)

    def sent(buf, count, sem):
        span = buf.at[pl.ds(0, count)]
        remote(span, span, sem, ra1.at[0], to_z[0]).wait_send()

    sent(bufa, NX - 1, sa1.at[0])
    sent(bufa, NX * long, sa2.at[0])
    sent(bufa, NX * short, sa2.at[1])
    sent(bufb, long, sb1.at[0])
    sent(bufb, short, sb1.at[1])
    sent(bufb, 3 * nz, sb2.at[0])
    for c in pending:
        c.wait_send()
    for j, p in zpeers:
        remote(send2.at[p], recv2.at[p], s2.at[p], r2.at[p], {"seq": x * nz + p}).wait_send()


def block(nz, ne, q, k, v, ld, sin, routes, gain, w_gate, w_up):
    tokens, width = q.shape
    heads, hd = ld.shape[0], sin.shape[1]
    rows = hd // nz
    _, hidden, depth = w_gate.shape
    units = NX * nz
    ka = depth * 22 // 48 // 128 * 128
    kb = depth + depth // 4 - ka
    dma = pltpu.SemaphoreType.DMA
    vmem = pl.BlockSpec(memory_space=pltpu.VMEM)
    return pl.pallas_call(
        functools.partial(block_kernel, nz, ne),
        out_shape=(
            jax.ShapeDtypeStruct((1, hidden, units * CAP), BF16),
            jax.ShapeDtypeStruct((heads, rows // NX, hd), F32),
        ),
        in_specs=[pl.BlockSpec(memory_space=pl.ANY)] * 9,
        out_specs=(vmem, vmem),
        scratch_shapes=[
            pltpu.VMEM(q.shape, BF16),
            pltpu.VMEM(k.shape, BF16),
            pltpu.VMEM(v.shape, BF16),
            pltpu.VMEM(ld.shape, F32),
            pltpu.VMEM(sin.shape, F32),
            pltpu.VMEM(routes.shape, jnp.int32),
            pltpu.VMEM(gain.shape, F32),
            pltpu.VMEM((2 * hidden, depth), BF16),
            pltpu.VMEM((nz, heads * rows, hd), F32),
            pltpu.VMEM((nz, heads * rows, hd), BF16),
            pltpu.VMEM((nz, heads * rows, hd), BF16),
            pltpu.VMEM((nz, 1, hd), F32),
            pltpu.VMEM((NX, heads * rows + 8, hd), F32),
            pltpu.VMEM((nz, heads * rows, hd), BF16),
            pltpu.VMEM((nz, heads * rows, hd), BF16),
            pltpu.VMEM((nz, heads * rows, hd), F32),
            pltpu.VMEM((tokens, width), F32),
            pltpu.VMEM((ne, 32, width), BF16),
            pltpu.VMEM((ne, 32, width), BF16),
            pltpu.VMEM((units, 16, ka), BF16),
            pltpu.VMEM((units, 16, kb), BF16),
            pltpu.VMEM((hidden, units * CAP), F32),
            dma((9,)),
            dma((nz,)),
            dma((nz,)),
            dma((nz,)),
            dma((nz,)),
            dma((NX,)),
            dma((NX,)),
            dma((nz,)),
            dma((nz,)),
            dma((ne,)),
            dma((ne,)),
            dma((1,)),
            dma((NX - 1,)),
            dma((2,)),
            dma((2, nz // 2, NX)),
            dma((2,)),
            dma((2, nz // 2)),
            dma((1,)),
            dma((3, 2 * nz)),
        ],
        compiler_params=pltpu.CompilerParams(
            collective_id=0, has_side_effects=True, vmem_limit_bytes=60 * 2**20
        ),
    )(q, k, v, ld, sin, routes, gain, w_gate, w_up)


def shards(nz, ne, queries, keys, values, log_decay, state_in, norm_gain, routes, w_gate, w_up):
    return block(
        nz, ne, queries, keys, values, log_decay, state_in, routes.T, norm_gain[None], w_gate, w_up
    )


def solution(mesh):
    placed = (
        P("seq", "exp"),
        P("seq", "exp"),
        P("seq", "exp"),
        P("exp", "seq"),
        P("exp", None, None),
        P(),
        P("seq", None),
        P("exp", "seq", None),
        P("exp", "seq", None),
    )
    return jax.shard_map(
        functools.partial(shards, mesh.shape["seq"] // NX, mesh.shape["exp"]),
        mesh=mesh,
        in_specs=placed,
        out_specs=(P("exp", "seq", None), P("exp", "seq", None)),
        check_vma=False,
    )
```

```python
import functools
import math

import jax
import jax.numpy as jnp
from jax import lax
from jax.experimental import pallas as pl
from jax.experimental.pallas import tpu as pltpu
from jax.sharding import PartitionSpec as P

MESH = pl.DeviceIdType.MESH
CAP = 20
EPSILON = 1e-06
NX = 4
HIGHEST = lax.Precision.HIGHEST
F32, BF16 = jnp.float32, jnp.bfloat16


def iota(shape, dim):
    return lax.broadcasted_iota(jnp.int32, shape, dim)


def dot(a, b, dims=((1,), (0,)), precision=None):
    return lax.dot_general(a, b, (dims, ((), ())), precision=precision, preferred_element_type=F32)


def remote(src, dst, send, recv, where):
    return pltpu.make_async_remote_copy(
        src_ref=src, dst_ref=dst, send_sem=send, recv_sem=recv, device_id=where, device_id_type=MESH
    )


def enter(peers):
    barrier = pltpu.get_barrier_semaphore()
    for peer in peers:
        pl.semaphore_signal(barrier, inc=1, device_id=peer, device_id_type=MESH)
    pl.semaphore_wait(barrier, len(peers))


def block_kernel(
    nz, ne, q_hbm, k_hbm, v_hbm, ld_hbm, sin_hbm, routes_hbm, gain_hbm, gate_hbm, up_hbm,
    out_ref, sout_ref,
    q_ref, k_ref, v_ref, ld_ref, sin_ref, routes_ref, gain_ref, wbuf,
    stage, send1, recv1, logs, xbuf, send2, recv2, ent, att, sende, recve, squares, whole_att, raw,
    bufa, bufb, tokb, acc,
    load, sl, rl, s1, r1, sx_sem, rx_sem, s2, r2, se, re, sq, rq, sr, rr,
    sa1, ra1, st1, rt1, sa2, ra2, st2, rt2, sb1, rb1, sb2, rb2, sy, ry, ss, rs,
):
    hidden = gate_hbm.shape[1]
    pairs = [
        (q_hbm, q_ref), (k_hbm, k_ref), (v_hbm, v_ref), (ld_hbm, ld_ref), (sin_hbm, sin_ref),
        (routes_hbm, routes_ref), (gain_hbm, gain_ref),
        (gate_hbm.at[0], wbuf.at[pl.ds(0, hidden)]), (up_hbm.at[0], wbuf.at[pl.ds(hidden, hidden)]),
    ]
    loads = [pltpu.make_async_copy(a, b, load.at[i]) for i, (a, b) in enumerate(pairs)]
    for c in loads:
        c.start()

    tokens = q_ref.shape[0]
    heads = ld_ref.shape[0]
    hd = sin_ref.shape[1]
    rows = hd // nz
    part = rows // NX
    width = heads * hd
    scaling = 1.0 / math.sqrt(hd)
    place = lax.axis_index("seq")
    x, z = place // nz, place % nz
    me = lax.axis_index("exp")
    far = sorted(range(1, nz), key=lambda j: -min(j, nz - j))
    zpeers = [(j, lax.rem(z + j, nz)) for j in far]
    xpeers = [(j, lax.rem(x + j, NX)) for j in range(1, NX)]
    epeers = [(j, lax.rem(me + j, ne)) for j in range(1, ne)]
    enter(
        [{"seq": x * nz + p} for _, p in zpeers]
        + [{"seq": p * nz + z} for _, p in xpeers]
        + [{"exp": p} for _, p in epeers]
    )
    for c in loads[:5]:
        c.wait()

    ld = ld_ref[...]
    at_or_before = (iota((tokens, tokens), 0) <= iota((tokens, tokens), 1)).astype(F32)
    causal = iota((tokens, tokens), 0) >= iota((tokens, tokens), 1)
    cum = dot(ld, at_or_before, precision=HIGHEST)
    cumt = dot(causal.astype(F32), ld, ((1,), (1,)), HIGHEST)
    lane = iota((1, hd), 1)
    total = jnp.zeros((1, hd), F32)
    for h in range(heads):
        total = jnp.where(lane == h, cumt[tokens - 1 : tokens, h : h + 1], total)
    logs[z] = total
    pending = []
    for j, p in zpeers:
        c = remote(logs.at[z], logs.at[z], sl.at[j], rl.at[j], {"seq": x * nz + p})
        c.start()
        pending.append(c)

    d = iota((hd, hd), 0)
    per_x = hd // NX
    order = (d % per_x) // part * rows + d // per_x * part + d % part
    perm = (order == iota((hd, hd), 1)).astype(BF16)

    def cols(h):
        return slice(h * hd, (h + 1) * hd)

    qs, ks = [], []
    for h in range(heads):
        ks.append(dot(k_ref[:, cols(h)], perm).astype(BF16))
    for h in range(heads):
        last = cum[h : h + 1, tokens - 1 : tokens]
        kw = ks[h].astype(F32) * jnp.exp(last - cumt[:, h : h + 1])
        high = kw.astype(BF16)
        low = (kw - high.astype(F32)).astype(BF16)
        vh = v_ref[:, cols(h)]
        state = dot(high, vh, ((0,), (0,))) + dot(low, vh, ((0,), (0,)))
        stage[:, h * rows : (h + 1) * rows, :] = state.reshape(nz, rows, hd)
    send1[...] = stage[...].astype(BF16)
    for j, p in zpeers:
        c = remote(send1.at[p], recv1.at[z], s1.at[j], r1.at[j], {"seq": x * nz + p})
        c.start()
        pending.append(c)
    recv1[z] = send1[z]

    for h in range(heads):
        qs.append(dot(q_ref[:, cols(h)], perm).astype(BF16))
        scores = dot(qs[h], ks[h], ((1,), (1,))) * scaling
        gap = cumt[:, h : h + 1] - cum[h : h + 1, :]
        weights = jnp.where(causal, jnp.exp(jnp.where(causal, gap, 0.0)), 0.0)
        att[:, cols(h)] = dot((scores * weights).astype(BF16), v_ref[:, cols(h)])

    pick_r, pick_d = iota((rows, hd), 0), iota((rows, hd), 1)
    pick = (pick_d == pick_r // part * per_x + z * part + pick_r % part).astype(F32)
    first = [dot(pick, sin_ref[h], precision=HIGHEST) for h in range(heads)]

    for c in loads[5:]:
        c.wait()
    expert = iota((ne, tokens), 0)
    chosen = (routes_ref[0:1, :] == expert) | (routes_ref[1:2, :] == expert)
    position = dot(chosen.astype(F32), at_or_before, precision=HIGHEST) - 1.0
    position = jnp.where(chosen, position, -1.0)
    line = iota((48, tokens), 0)
    group = (2 * me + line // 32) // 3
    slot = jnp.where(line < 16, line, jnp.where(line % 16 // 4 == group, 16 + line % 4, -5))
    slot = slot.astype(F32)
    selectors = [
        (jnp.abs(slot - position[e : e + 1, :]) < 0.5).astype(F32).astype(BF16) for e in range(ne)
    ]
    slots = jnp.sum(jnp.where(expert == me, position, 0.0), axis=0, keepdims=True)
    acc[...] = jnp.zeros_like(acc)

    for j, p in zpeers:
        src = lax.rem(z + nz - j, nz)
        remote(logs.at[src], logs.at[src], sl.at[j], rl.at[j], {"seq": x * nz + src}).wait_recv()
    decays = [jnp.exp(logs[j]) for j in range(nz)]
    whole = sum([logs[j] for j in range(nz)])
    for j, p in zpeers:
        src = lax.rem(z + nz - j, nz)
        remote(send1.at[src], recv1.at[src], s1.at[j], r1.at[j], {"seq": x * nz + src}).wait_recv()

    def step(running, piece, decay):
        return [
            decay[0:1, h : h + 1] * running[h] + piece[h * rows : (h + 1) * rows]
            for h in range(heads)
        ]

    srows = heads * rows
    running = [jnp.zeros((rows, hd), F32)] * heads
    for j in range(nz):
        running = step(running, recv1[j].astype(F32), decays[j])
    for h in range(heads):
        xbuf[x, h * rows : (h + 1) * rows, :] = running[h]
    xbuf[x, srows : srows + 8, :] = jnp.broadcast_to(whole, (8, hd))
    for j, p in xpeers:
        c = remote(xbuf.at[x], xbuf.at[x], sx_sem.at[j], rx_sem.at[j], {"seq": p * nz + z})
        c.start()
        pending.append(c)
    for j, p in xpeers:
        src = lax.rem(x + NX - j, NX)
        remote(
            xbuf.at[src], xbuf.at[src], sx_sem.at[j], rx_sem.at[j], {"seq": src * nz + z}
        ).wait_recv()

    final = first
    entering = first
    for g in range(NX):
        entering = [jnp.where(x == g, f, e) for f, e in zip(final, entering)]
        final = step(final, xbuf[g], jnp.exp(xbuf[g, srows : srows + 8, :]))
    for j in range(nz):
        send2[j] = jnp.concatenate(entering, axis=0).astype(BF16)

        @pl.when(z != j)
        def _(j=j):
            remote(send2.at[j], recv2.at[z], s2.at[j], r2.at[z], {"seq": x * nz + j}).start()

        if j < nz - 1:
            entering = step(entering, recv1[j].astype(F32), decays[j])
    recv2[z] = send2[z]
    for h in range(heads):
        mine = jnp.zeros((part, hd), F32)
        for g in range(NX):
            mine = jnp.where(x == g, final[h][g * part : (g + 1) * part], mine)
        sout_ref[h] = mine
    for j, p in zpeers:
        remote(send2.at[p], recv2.at[p], s2.at[p], r2.at[p], {"seq": x * nz + p}).wait_recv()

    ent[...] = recv2[...].astype(F32)
    parts = []
    for h in range(heads):
        state = ent[:, h * rows : (h + 1) * rows, :].reshape(hd, hd).astype(BF16)
        carried = dot(qs[h], state) * scaling * jnp.exp(cumt[:, h : h + 1])
        parts.append((att[:, cols(h)] + carried).astype(BF16))
    attended = jnp.concatenate(parts, axis=1)
    y, core = me // 2, me % 2
    by_rows = ne - 2
    wide = attended.astype(F32)
    square = dot(jnp.ones((8, width), F32), wide * wide, ((1,), (1,)), HIGHEST)[0:1]
    squares[me] = jnp.concatenate([square, jnp.zeros((1, hd - tokens), F32)], axis=1)
    for j, p in epeers:
        c = remote(squares.at[me], squares.at[me], sq.at[j], rq.at[j], {"exp": p})
        c.start()
        pending.append(c)
    ny = ne // 2
    whole_att[...] = attended.reshape(ny, tokens // ny, width)

    def raw_to(t):
        return remote(whole_att.at[t], raw.at[0], sr.at[t], rr.at[0], {"exp": 2 * t + core})

    @pl.when(me >= by_rows)
    def _():
        for t in range(ny - 1):
            raw_to(t).start()
        raw[0] = whole_att[ny - 1]

    half = width // 2
    for e in range(ne):
        picked = dot(selectors[e], attended).astype(BF16)
        last = jnp.concatenate([picked[16:32, 0:half], picked[32:48, half:width]], axis=1)
        sende[e] = jnp.concatenate([picked[0:16], last], axis=0)

    def rows_to(j, p):
        return remote(sende.at[p], recve.at[me], se.at[j], re.at[me], {"exp": p})

    @pl.when(me < by_rows)
    def _():
        for j, p in epeers:
            rows_to(j, p).start()
        recve[me] = sende[me]

    for j, p in epeers:
        src = lax.rem(me + ne - j, ne)
        remote(squares.at[src], squares.at[src], sq.at[j], rq.at[j], {"exp": src}).wait_recv()

    depth = ne * width
    deep = by_rows * width
    quarter = deep // 4
    ka = bufa.shape[2] - 128
    own = z * NX + x
    square = sum([squares[e] for e in range(ne)])[:, 0:tokens]
    scale = lax.rsqrt(square / depth + EPSILON)
    line = iota((32, tokens), 0)
    slot = jnp.where(line < 16, line, 16 + line % 4).astype(F32)
    hit = jnp.abs(slot - slots) < 0.5
    row_scale = jnp.sum(jnp.where(hit, scale, 0.0), axis=1, keepdims=True)
    line = iota((16, tokens), 0)
    hit = iota((16, tokens), 1) == y * 16 + line
    tok_scale = jnp.sum(jnp.where(hit, scale, 0.0), axis=1, keepdims=True)

    lane = iota((tokens, NX * tokens), 1)
    spot = (lane // 16 % NX == x) & (lane // (16 * NX) * 16 + lane % 16 == iota(lane.shape, 0))
    named = jnp.broadcast_to((slots + 1.0).astype(BF16), (16, tokens))
    named = dot(named, spot.astype(F32).astype(BF16))
    line = iota((16, 128), 0)
    named = jnp.where(line == 0, named[:, 0:128], jnp.where(line == 1, named[:, 128:256], 0.0))
    bufa[own, :, ka : ka + 128] = named.astype(BF16)

    @pl.when(me < by_rows)
    def _():
        remote(raw.at[0], raw.at[0], sr.at[0], rr.at[0], {"exp": by_rows + core}).wait_recv()

    at = depth - 2 * width
    gain = jnp.where(
        core == 0, gain_ref[:, at : at + width], gain_ref[:, at + width : at + 2 * width]
    )
    tokb[core * ny + y, own] = (raw[0].astype(F32) * tok_scale * gain).astype(BF16)

    for src in range(by_rows):

        @pl.when(me != src)
        def _(src=src):
            remote(recve.at[src], recve.at[src], se.at[0], re.at[src], {"exp": src}).wait_recv()

    def put(start, value):
        if start < ka:
            bufa[own, :, start : start + value.shape[1]] = value
        else:
            bufb[own, :, start - ka : start - ka + value.shape[1]] = value

    for e in range(by_rows):
        gain = gain_ref[:, e * width : (e + 1) * width]
        put(e * width, (recve[e, 0:16].astype(F32) * row_scale[0:16] * gain).astype(BF16))
    line = iota((16, half), 0) // 4
    for i in range(3):
        gain = jnp.zeros((16, half), F32)
        rest = jnp.zeros((16, half), F32)
        for g in range(4):
            at = g * quarter + i * half
            gain = jnp.where(line == g, gain_ref[:, at : at + half], gain)
            e, side = (3 * g + i) // 2, (3 * g + i) % 2 * half
            rest = rest + recve[e, 16:32, side : side + half].astype(F32)
        put(deep + i * half, (rest * row_scale[16:32] * gain).astype(BF16))

    long, short = nz // 2, nz - 1 - nz // 2
    d = 1 - 2 * core

    def zat(k):
        return lax.rem(z + k * d + 2 * nz, nz)

    def xat(k):
        return lax.rem(x + k * d + 2 * NX, NX)

    to_z = [{"seq": x * nz + zat(1)}, {"seq": x * nz + zat(-1)}]
    to_x = [{"seq": xat(j) * nz + z} for j in range(NX)]

    to_y = [{"exp": lax.rem(y + j * d + ny, ny) * 2 + core} for j in (1, -1)]
    sibling = {"exp": me + d}

    def columns(o):
        return pl.ds(zat(o) * NX, NX)

    def a1(j, back):
        u = z * NX + xat(-back)
        return remote(bufa.at[u], bufa.at[u], sa1.at[0], ra1.at[j - 1], to_x[j])

    def t1(j, back):
        part = tokb.at[core * ny + y, z * NX + xat(-back)]
        return remote(part, part, st1.at[0], rt1.at[j - 1], to_x[j])

    def a2(way, k, c, ahead=0):
        u = zat(-k - ahead if way == 0 else k + ahead) * NX + xat(-c)
        return remote(bufa.at[u], bufa.at[u], sa2.at[way], ra2.at[way, k, c], to_z[way])

    def t2(way, k, c, ahead=0):
        u = zat(-k - ahead if way == 0 else k + ahead) * NX + xat(-c)
        part = tokb.at[core * ny + y, u]
        return remote(part, part, st2.at[way], rt2.at[way, k, c], to_z[way])

    def tok_y(o, kind, back):
        part = tokb.at[core * ny + lax.rem(y - back * d + 2 * ny, ny), columns(o)]
        return remote(part, part, sy.at[0], ry.at[kind, o + nz], to_y[1 if kind == 1 else 0])

    def tok_core(o, whose):
        part = tokb.at[pl.ds(whose * ny, ny), columns(o)]
        return remote(part, part, ss.at[0], rs.at[o + nz], sibling)

    def y_spread(o):
        tok_y(o, 0, 0).start()
        tok_y(o, 1, 0).start()

    def y_forward(o):
        tok_y(o, 0, 1).wait_recv()
        tok_y(o, 2, 1).start()

    def y_share(o):
        tok_y(o, 1, -1).wait_recv()
        tok_y(o, 2, 2).wait_recv()
        tok_core(o, core).start()

    def b1(way, k):
        u = zat(-k if way == 0 else k) * NX + x
        return remote(bufb.at[u], bufb.at[u], sb1.at[way], rb1.at[way, k], to_z[way])

    def b1_arrived(way, k):
        u = zat(-k - 1 if way == 0 else k + 1) * NX + x
        return remote(bufb.at[u], bufb.at[u], sb1.at[way], rb1.at[way, k], to_z[way])

    def b2(o, kind):
        u = zat(o) * NX + (x if kind < 2 else xat(-1))
        where = to_x[NX - 1] if kind == 1 else to_x[1]
        return remote(bufb.at[u], bufb.at[u], sb2.at[0], rb2.at[kind, o + nz], where)

    def b2_arrived(o, kind):
        u = zat(o) * NX + xat((-1, 1, -2)[kind])
        where = to_x[NX - 1] if kind == 1 else to_x[1]
        return remote(bufb.at[u], bufb.at[u], sb2.at[0], rb2.at[kind, o + nz], where)

    def spread(o):
        b2(o, 0).start()
        b2(o, 1).start()

    def forward(o):
        b2_arrived(o, 0).wait_recv()
        b2(o, 2).start()

    def finish(o):
        b2_arrived(o, 1).wait_recv()
        b2_arrived(o, 2).wait_recv()
        tok_core(o, 1 - core).wait_recv()

    lanes = 16 * NX

    def compute(offsets):
        n = lanes * len(offsets)
        zs = [zat(o) for o in offsets]

        def stacked(buf, start, size):
            got = [
                buf[pl.ds(zz * NX, NX), :, start : start + size].reshape(lanes, size) for zz in zs
            ]
            return got[0] if len(got) == 1 else jnp.concatenate(got, axis=0)

        t = ((1,), (1,))
        main = dot(wbuf[:, 0:ka], stacked(bufa, 0, ka), t)
        main = main + dot(wbuf[:, ka:deep], stacked(bufb, 0, deep - ka), t)
        tail = stacked(bufb, deep - ka, quarter)
        lane = iota((2 * hidden, n), 1)
        rest = jnp.zeros((2 * hidden, n), F32)
        for g in range(4):
            one = dot(wbuf[:, g * quarter : (g + 1) * quarter], tail, t)
            rest = rest + jnp.where(lane % 16 // 4 == g, one, 0.0)
        span = NX * tokens
        line, key = iota((2 * lanes, span), 0), iota((2 * lanes, span), 1)
        r = line % 16
        want = jnp.where(line < lanes, r + 1, jnp.where(r >= 12, r + 5, -5))
        want = jnp.where(line % lanes // 16 == key // 16 % NX, want, -5).astype(F32)
        picked = [[], []]
        for zz in zs:
            tile = bufa[pl.ds(zz * NX, NX), :, ka : ka + 128].astype(F32).sum(axis=0)
            named = jnp.concatenate([tile[0:1], tile[1:2]], axis=1)
            pick = (jnp.abs(want - named) < 0.5).astype(F32).astype(BF16)
            for i in range(2):
                source = jnp.concatenate(
                    [
                        tokb[i * ny + t, pl.ds(zz * NX, NX)].reshape(NX * 16, width)
                        for t in range(ny)
                    ],
                    axis=0,
                )
                picked[i].append(dot(pick, source).astype(BF16))
        for i in range(2):
            w = wbuf[:, deep + i * width : deep + (i + 1) * width]
            main = main + dot(w, jnp.concatenate([p[0:lanes] for p in picked[i]], axis=0), t)
            rest = rest + dot(w, jnp.concatenate([p[lanes:] for p in picked[i]], axis=0), t)
        if n < 128:
            rest = jnp.concatenate([rest, jnp.zeros((2 * hidden, 128 - n), F32)], axis=1)
            main = jnp.concatenate([main, jnp.zeros((2 * hidden, 128 - n), F32)], axis=1)
        rest = sum([pltpu.roll(rest, 4 * g, 1) for g in range(1, 4)], rest)

        def gated(a):
            gate, up = a[0:hidden], a[hidden : 2 * hidden]
            return (gate / (1.0 + jnp.exp(-gate)) * up).astype(BF16)

        columns = acc.shape[1]
        l = iota((128, columns), 0)
        r = l % 16
        start = zs[0] * CAP if len(zs) == 1 else jnp.where(l < lanes, zs[0], zs[1]) * CAP
        start = start + l % lanes // 16 * (nz * CAP)
        n_at = iota((128, columns), 1)
        used = l < n
        p_main = ((n_at == start + r) & used).astype(F32).astype(BF16)
        p_rest = ((n_at == start + 16 + r % 4) & (r >= 12) & used).astype(F32).astype(BF16)
        acc[...] += dot(gated(main), p_main) + dot(gated(rest), p_rest)

    spread(0)
    for j in (1, 3, 2):
        t1(j, 0).start()
    for way in range(2):
        b1(way, 0).start()
        t2(way, 0, 0).start()
        a2(way, 0, 0).start()
    for j in (1, 3, 2):
        a1(j, 0).start()
    for j in (1, 3, 2):
        t1(j, j).wait_recv()
        for way in range(2):
            t2(way, 0, j).start()
    y_spread(0)
    for j in (1, 3, 2):
        a1(j, j).wait_recv()
        for way in range(2):
            a2(way, 0, j).start()
    for way, o in ((0, -1), (1, 1)):
        b1_arrived(way, 0).wait_recv()
        b1(way, 1).start()
        spread(o)
    for c in (0, 1, 3, 2):
        for way in range(2):
            t2(way, 0, c, 1).wait_recv()
            t2(way, 1, c).start()
    y_spread(-1)
    y_spread(1)
    forward(0)
    y_forward(0)

    def turn(t, first=False, both=True, ahead=(True, True)):
        ways = (0, 1) if both else (0,)
        for c in (0, 1, 3, 2):
            for way in ways:
                t2(way, t, c, 1).wait_recv()
                if ahead[way]:
                    t2(way, t + 1, c).start()
        for way in ways:
            y_spread(-t - 1 if way == 0 else t + 1)
        for way in ways:
            o = -t - 1 if way == 0 else t + 1
            b1_arrived(way, t).wait_recv()
            if ahead[way]:
                b1(way, t + 1).start()
            spread(o)
        for c in (0, 1, 3, 2):
            for way in range(2):
                a2(way, t - 1, c, 1).wait_recv()
                if way in ways:
                    a2(way, t, c).start()
        for o in (-t, t):
            forward(o)
            y_forward(o)
        if first:
            y_share(0)
            finish(0)
            compute([0])
        else:
            finish(1 - t)
            finish(t - 1)
            compute([1 - t, t - 1])
        y_share(-t)
        y_share(t)

    turn(1, first=True)

    @pl.loop(2, short - 1)
    def _(t):
        turn(t)

    turn(short - 1, ahead=(True, False))
    turn(long - 1, both=False, ahead=(False, False))
    forward(-long)
    y_forward(-long)
    finish(1 - long)
    finish(long - 1)
    compute([1 - long, long - 1])
    y_share(-long)
    for c in (0, 1, 3, 2):
        a2(0, long - 1, c, 1).wait_recv()
    finish(-long)
    compute([-long])
    out_ref[0] = acc[...].astype(BF16)

    def sent(buf, count, sem):
        span = buf.at[pl.ds(0, count)]
        remote(span, span, sem, ra1.at[0], to_z[0]).wait_send()

    sent(bufa, NX - 1, sa1.at[0])
    sent(tokb.at[0], NX - 1, st1.at[0])
    for way, count in ((0, long), (1, short)):
        sent(bufa, NX * count, sa2.at[way])
        sent(tokb.at[0], NX * count, st2.at[way])
    sent(tokb, 3, sy.at[0])
    sent(tokb, ny, ss.at[0])
    sent(bufb, long, sb1.at[0])
    sent(bufb, short, sb1.at[1])
    sent(bufb, 3 * nz, sb2.at[0])
    for c in pending:
        c.wait_send()
    for j, p in zpeers:
        remote(send2.at[p], recv2.at[p], s2.at[p], r2.at[p], {"seq": x * nz + p}).wait_send()

    @pl.when(me >= by_rows)
    def _():
        for t in range(ny - 1):
            raw_to(t).wait_send()

    @pl.when(me < by_rows)
    def _():
        for j, p in epeers:
            rows_to(j, p).wait_send()


def block(nz, ne, q, k, v, ld, sin, routes, gain, w_gate, w_up):
    tokens, width = q.shape
    heads, hd = ld.shape[0], sin.shape[1]
    rows = hd // nz
    _, hidden, depth = w_gate.shape
    units = NX * nz
    deep = depth - 2 * width
    ka = 2 * width
    kb = deep + deep // 4 - ka
    dma = pltpu.SemaphoreType.DMA
    vmem = pl.BlockSpec(memory_space=pltpu.VMEM)
    return pl.pallas_call(
        functools.partial(block_kernel, nz, ne),
        out_shape=(
            jax.ShapeDtypeStruct((1, hidden, units * CAP), BF16),
            jax.ShapeDtypeStruct((heads, rows // NX, hd), F32),
        ),
        in_specs=[pl.BlockSpec(memory_space=pl.ANY)] * 9,
        out_specs=(vmem, vmem),
        scratch_shapes=[
            pltpu.VMEM(q.shape, BF16),
            pltpu.VMEM(k.shape, BF16),
            pltpu.VMEM(v.shape, BF16),
            pltpu.VMEM(ld.shape, F32),
            pltpu.VMEM(sin.shape, F32),
            pltpu.VMEM(routes.shape, jnp.int32),
            pltpu.VMEM(gain.shape, F32),
            pltpu.VMEM((2 * hidden, depth), BF16),
            pltpu.VMEM((nz, heads * rows, hd), F32),
            pltpu.VMEM((nz, heads * rows, hd), BF16),
            pltpu.VMEM((nz, heads * rows, hd), BF16),
            pltpu.VMEM((nz, 1, hd), F32),
            pltpu.VMEM((NX, heads * rows + 8, hd), F32),
            pltpu.VMEM((nz, heads * rows, hd), BF16),
            pltpu.VMEM((nz, heads * rows, hd), BF16),
            pltpu.VMEM((nz, heads * rows, hd), F32),
            pltpu.VMEM((tokens, width), F32),
            pltpu.VMEM((ne, 32, width), BF16),
            pltpu.VMEM((ne, 32, width), BF16),
            pltpu.VMEM((ne, 1, hd), F32),
            pltpu.VMEM((ne // 2, 16, width), BF16),
            pltpu.VMEM((1, 16, width), BF16),
            pltpu.VMEM((units, 16, ka + 128), BF16),
            pltpu.VMEM((units, 16, kb), BF16),
            pltpu.VMEM((ne, units, 16, width), BF16),
            pltpu.VMEM((hidden, units * CAP), F32),
            dma((9,)),
            dma((nz,)),
            dma((nz,)),
            dma((nz,)),
            dma((nz,)),
            dma((NX,)),
            dma((NX,)),
            dma((nz,)),
            dma((nz,)),
            dma((ne,)),
            dma((ne,)),
            dma((ne,)),
            dma((ne,)),
            dma((ne // 2,)),
            dma((1,)),
            dma((1,)),
            dma((NX - 1,)),
            dma((1,)),
            dma((NX - 1,)),
            dma((2,)),
            dma((2, nz // 2, NX)),
            dma((2,)),
            dma((2, nz // 2, NX)),
            dma((2,)),
            dma((2, nz // 2)),
            dma((1,)),
            dma((3, 2 * nz)),
            dma((1,)),
            dma((3, 2 * nz)),
            dma((1,)),
            dma((2 * nz,)),
        ],
        compiler_params=pltpu.CompilerParams(
            collective_id=0, has_side_effects=True, vmem_limit_bytes=60 * 2**20
        ),
    )(q, k, v, ld, sin, routes, gain, w_gate, w_up)


def shards(nz, ne, queries, keys, values, log_decay, state_in, norm_gain, routes, w_gate, w_up):
    return block(
        nz, ne, queries, keys, values, log_decay, state_in, routes.T, norm_gain[None], w_gate, w_up
    )


def solution(mesh):
    placed = (
        P("seq", "exp"),
        P("seq", "exp"),
        P("seq", "exp"),
        P("exp", "seq"),
        P("exp", None, None),
        P(),
        P("seq", None),
        P("exp", "seq", None),
        P("exp", "seq", None),
    )
    return jax.shard_map(
        functools.partial(shards, mesh.shape["seq"] // NX, mesh.shape["exp"]),
        mesh=mesh,
        in_specs=placed,
        out_specs=(P("exp", "seq", None), P("exp", "seq", None)),
        check_vma=False,
    )
```

```python
import functools
import math

import jax
import jax.numpy as jnp
from jax import lax
from jax.experimental import pallas as pl
from jax.experimental.pallas import tpu as pltpu
from jax.sharding import PartitionSpec as P

MESH = pl.DeviceIdType.MESH
CAP = 20
EPSILON = 1e-06
NX = 4
HIGHEST = lax.Precision.HIGHEST
F32, BF16 = jnp.float32, jnp.bfloat16


def iota(shape, dim):
    return lax.broadcasted_iota(jnp.int32, shape, dim)


def dot(a, b, dims=((1,), (0,)), precision=None):
    return lax.dot_general(a, b, (dims, ((), ())), precision=precision, preferred_element_type=F32)


def remote(src, dst, send, recv, where):
    return pltpu.make_async_remote_copy(
        src_ref=src, dst_ref=dst, send_sem=send, recv_sem=recv, device_id=where, device_id_type=MESH
    )


def enter(peers):
    barrier = pltpu.get_barrier_semaphore()
    for peer in peers:
        pl.semaphore_signal(barrier, inc=1, device_id=peer, device_id_type=MESH)
    pl.semaphore_wait(barrier, len(peers))


def block_kernel(
    nz, ne, q_hbm, k_hbm, v_hbm, ld_hbm, sin_hbm, routes_hbm, gain_hbm, gate_hbm, up_hbm,
    out_ref, sout_ref,
    q_ref, k_ref, v_ref, ld_ref, sin_ref, routes_ref, gain_ref, wbuf,
    stage, send1, recv1, logs, xbuf, send2, recv2, ent, att, sende, recve, squares, whole_att, raw,
    bufa, bufb, tokb, acc,
    load, sl, rl, s1, r1, sx_sem, rx_sem, s2, r2, se, re, sq, rq, sr, rr,
    sa1, ra1, st1, rt1, sa2, ra2, st2, rt2, sb1, rb1, sb2, rb2, sy, ry, ss, rs,
):
    hidden = gate_hbm.shape[1]
    pairs = [
        (q_hbm, q_ref), (k_hbm, k_ref), (v_hbm, v_ref), (ld_hbm, ld_ref), (sin_hbm, sin_ref),
        (routes_hbm, routes_ref), (gain_hbm, gain_ref),
        (gate_hbm.at[0], wbuf.at[pl.ds(0, hidden)]), (up_hbm.at[0], wbuf.at[pl.ds(hidden, hidden)]),
    ]
    loads = [pltpu.make_async_copy(a, b, load.at[i]) for i, (a, b) in enumerate(pairs)]
    for c in loads:
        c.start()

    tokens = q_ref.shape[0]
    heads = ld_ref.shape[0]
    hd = sin_ref.shape[1]
    rows = hd // nz
    part = rows // NX
    width = heads * hd
    scaling = 1.0 / math.sqrt(hd)
    place = lax.axis_index("seq")
    x, z = place // nz, place % nz
    me = lax.axis_index("exp")
    far = sorted(range(1, nz), key=lambda j: -min(j, nz - j))
    zpeers = [(j, lax.rem(z + j, nz)) for j in far]
    xpeers = [(j, lax.rem(x + j, NX)) for j in range(1, NX)]
    epeers = [(j, lax.rem(me + j, ne)) for j in range(1, ne)]
    enter(
        [{"seq": x * nz + p} for _, p in zpeers]
        + [{"seq": p * nz + z} for _, p in xpeers]
        + [{"exp": p} for _, p in epeers]
    )
    for c in loads[:5]:
        c.wait()

    ld = ld_ref[...]
    at_or_before = (iota((tokens, tokens), 0) <= iota((tokens, tokens), 1)).astype(F32)
    causal = iota((tokens, tokens), 0) >= iota((tokens, tokens), 1)
    cum = dot(ld, at_or_before, precision=HIGHEST)
    cumt = dot(causal.astype(F32), ld, ((1,), (1,)), HIGHEST)
    lane = iota((1, hd), 1)
    total = jnp.zeros((1, hd), F32)
    for h in range(heads):
        total = jnp.where(lane == h, cumt[tokens - 1 : tokens, h : h + 1], total)
    logs[z] = total
    pending = []
    for j, p in zpeers:
        c = remote(logs.at[z], logs.at[z], sl.at[j], rl.at[j], {"seq": x * nz + p})
        c.start()
        pending.append(c)

    d = iota((hd, hd), 0)
    per_x = hd // NX
    order = (d % per_x) // part * rows + d // per_x * part + d % part
    perm = (order == iota((hd, hd), 1)).astype(BF16)

    def cols(h):
        return slice(h * hd, (h + 1) * hd)

    qs, ks = [], []
    for h in range(heads):
        ks.append(dot(k_ref[:, cols(h)], perm).astype(BF16))
    for h in range(heads):
        last = cum[h : h + 1, tokens - 1 : tokens]
        kw = ks[h].astype(F32) * jnp.exp(last - cumt[:, h : h + 1])
        high = kw.astype(BF16)
        low = (kw - high.astype(F32)).astype(BF16)
        vh = v_ref[:, cols(h)]
        state = dot(high, vh, ((0,), (0,))) + dot(low, vh, ((0,), (0,)))
        stage[:, h * rows : (h + 1) * rows, :] = state.reshape(nz, rows, hd)
    send1[...] = stage[...].astype(BF16)
    for j, p in zpeers:
        c = remote(send1.at[p], recv1.at[z], s1.at[j], r1.at[j], {"seq": x * nz + p})
        c.start()
        pending.append(c)
    recv1[z] = send1[z]

    for h in range(heads):
        qs.append(dot(q_ref[:, cols(h)], perm).astype(BF16))
        scores = dot(qs[h], ks[h], ((1,), (1,))) * scaling
        gap = cumt[:, h : h + 1] - cum[h : h + 1, :]
        weights = jnp.where(causal, jnp.exp(jnp.where(causal, gap, 0.0)), 0.0)
        att[:, cols(h)] = dot((scores * weights).astype(BF16), v_ref[:, cols(h)])

    pick_r, pick_d = iota((rows, hd), 0), iota((rows, hd), 1)
    pick = (pick_d == pick_r // part * per_x + z * part + pick_r % part).astype(F32)
    first = [dot(pick, sin_ref[h], precision=HIGHEST) for h in range(heads)]

    for c in loads[5:]:
        c.wait()
    expert = iota((ne, tokens), 0)
    chosen = (routes_ref[0:1, :] == expert) | (routes_ref[1:2, :] == expert)
    position = dot(chosen.astype(F32), at_or_before, precision=HIGHEST) - 1.0
    position = jnp.where(chosen, position, -1.0)
    line = iota((48, tokens), 0)
    group = (2 * me + line // 32) // 3
    slot = jnp.where(line < 16, line, jnp.where(line % 16 // 4 == group, 16 + line % 4, -5))
    slot = slot.astype(F32)
    selectors = [
        (jnp.abs(slot - position[e : e + 1, :]) < 0.5).astype(F32).astype(BF16) for e in range(ne)
    ]
    slots = jnp.sum(jnp.where(expert == me, position, 0.0), axis=0, keepdims=True)
    acc[...] = jnp.zeros_like(acc)

    for j, p in zpeers:
        src = lax.rem(z + nz - j, nz)
        remote(logs.at[src], logs.at[src], sl.at[j], rl.at[j], {"seq": x * nz + src}).wait_recv()
    decays = [jnp.exp(logs[j]) for j in range(nz)]
    whole = sum([logs[j] for j in range(nz)])
    for j, p in zpeers:
        src = lax.rem(z + nz - j, nz)
        remote(send1.at[src], recv1.at[src], s1.at[j], r1.at[j], {"seq": x * nz + src}).wait_recv()

    def step(running, piece, decay):
        return [
            decay[0:1, h : h + 1] * running[h] + piece[h * rows : (h + 1) * rows]
            for h in range(heads)
        ]

    srows = heads * rows
    running = [jnp.zeros((rows, hd), F32)] * heads
    for j in range(nz):
        running = step(running, recv1[j].astype(F32), decays[j])
    for h in range(heads):
        xbuf[x, h * rows : (h + 1) * rows, :] = running[h]
    xbuf[x, srows : srows + 8, :] = jnp.broadcast_to(whole, (8, hd))
    for j, p in xpeers:
        c = remote(xbuf.at[x], xbuf.at[x], sx_sem.at[j], rx_sem.at[j], {"seq": p * nz + z})
        c.start()
        pending.append(c)
    for j, p in xpeers:
        src = lax.rem(x + NX - j, NX)
        remote(
            xbuf.at[src], xbuf.at[src], sx_sem.at[j], rx_sem.at[j], {"seq": src * nz + z}
        ).wait_recv()

    final = first
    entering = first
    for g in range(NX):
        entering = [jnp.where(x == g, f, e) for f, e in zip(final, entering)]
        final = step(final, xbuf[g], jnp.exp(xbuf[g, srows : srows + 8, :]))
    for j in range(nz):
        send2[j] = jnp.concatenate(entering, axis=0).astype(BF16)

        @pl.when(z != j)
        def _(j=j):
            remote(send2.at[j], recv2.at[z], s2.at[j], r2.at[z], {"seq": x * nz + j}).start()

        if j < nz - 1:
            entering = step(entering, recv1[j].astype(F32), decays[j])
    recv2[z] = send2[z]
    for h in range(heads):
        mine = jnp.zeros((part, hd), F32)
        for g in range(NX):
            mine = jnp.where(x == g, final[h][g * part : (g + 1) * part], mine)
        sout_ref[h] = mine
    for j, p in zpeers:
        remote(send2.at[p], recv2.at[p], s2.at[p], r2.at[p], {"seq": x * nz + p}).wait_recv()

    ent[...] = recv2[...].astype(F32)
    parts = []
    for h in range(heads):
        state = ent[:, h * rows : (h + 1) * rows, :].reshape(hd, hd).astype(BF16)
        carried = dot(qs[h], state) * scaling * jnp.exp(cumt[:, h : h + 1])
        parts.append((att[:, cols(h)] + carried).astype(BF16))
    attended = jnp.concatenate(parts, axis=1)
    y, core = me // 2, me % 2
    by_rows = ne - 2
    wide = attended.astype(F32)
    square = dot(jnp.ones((8, width), F32), wide * wide, ((1,), (1,)), HIGHEST)[0:1]
    squares[me] = jnp.concatenate([square, jnp.zeros((1, hd - tokens), F32)], axis=1)
    for j, p in epeers:
        c = remote(squares.at[me], squares.at[me], sq.at[j], rq.at[j], {"exp": p})
        c.start()
        pending.append(c)
    ny = ne // 2
    whole_att[...] = attended.reshape(ny, tokens // ny, width)

    def raw_to(t):
        return remote(whole_att.at[t], raw.at[0], sr.at[t], rr.at[0], {"exp": 2 * t + core})

    @pl.when(me >= by_rows)
    def _():
        for t in range(ny - 1):
            raw_to(t).start()
        raw[0] = whole_att[ny - 1]

    half = width // 2
    for e in range(ne):
        picked = dot(selectors[e], attended).astype(BF16)
        last = jnp.concatenate([picked[16:32, 0:half], picked[32:48, half:width]], axis=1)
        sende[e] = jnp.concatenate([picked[0:16], last], axis=0)

    def rows_to(j, p):
        return remote(sende.at[p], recve.at[me], se.at[j], re.at[me], {"exp": p})

    @pl.when(me < by_rows)
    def _():
        for j, p in epeers:
            rows_to(j, p).start()
        recve[me] = sende[me]

    for j, p in epeers:
        src = lax.rem(me + ne - j, ne)
        remote(squares.at[src], squares.at[src], sq.at[j], rq.at[j], {"exp": src}).wait_recv()

    depth = ne * width
    deep = by_rows * width
    quarter = deep // 4
    ka = bufa.shape[2] - 128
    own = z * NX + x
    square = sum([squares[e] for e in range(ne)])[:, 0:tokens]
    scale = lax.rsqrt(square / depth + EPSILON)
    line = iota((32, tokens), 0)
    slot = jnp.where(line < 16, line, 16 + line % 4).astype(F32)
    hit = jnp.abs(slot - slots) < 0.5
    row_scale = jnp.sum(jnp.where(hit, scale, 0.0), axis=1, keepdims=True)
    line = iota((16, tokens), 0)
    hit = iota((16, tokens), 1) == y * 16 + line
    tok_scale = jnp.sum(jnp.where(hit, scale, 0.0), axis=1, keepdims=True)

    lane = iota((tokens, NX * tokens), 1)
    spot = (lane // 16 % NX == x) & (lane // (16 * NX) * 16 + lane % 16 == iota(lane.shape, 0))
    named = jnp.broadcast_to((slots + 1.0).astype(BF16), (16, tokens))
    named = dot(named, spot.astype(F32).astype(BF16))
    line = iota((16, 128), 0)
    named = jnp.where(line == 0, named[:, 0:128], jnp.where(line == 1, named[:, 128:256], 0.0))
    bufa[own, :, ka : ka + 128] = named.astype(BF16)

    @pl.when(me < by_rows)
    def _():
        remote(raw.at[0], raw.at[0], sr.at[0], rr.at[0], {"exp": by_rows + core}).wait_recv()

    at = depth - 2 * width
    gain = jnp.where(
        core == 0, gain_ref[:, at : at + width], gain_ref[:, at + width : at + 2 * width]
    )
    tokb[core * ny + y, own] = (raw[0].astype(F32) * tok_scale * gain).astype(BF16)

    for src in range(by_rows):

        @pl.when(me != src)
        def _(src=src):
            remote(recve.at[src], recve.at[src], se.at[0], re.at[src], {"exp": src}).wait_recv()

    def put(start, value):
        if start < ka:
            bufa[own, :, start : start + value.shape[1]] = value
        else:
            bufb[own, :, start - ka : start - ka + value.shape[1]] = value

    for e in range(by_rows):
        gain = gain_ref[:, e * width : (e + 1) * width]
        put(e * width, (recve[e, 0:16].astype(F32) * row_scale[0:16] * gain).astype(BF16))
    line = iota((16, half), 0) // 4
    for i in range(3):
        gain = jnp.zeros((16, half), F32)
        rest = jnp.zeros((16, half), F32)
        for g in range(4):
            at = g * quarter + i * half
            gain = jnp.where(line == g, gain_ref[:, at : at + half], gain)
            e, side = (3 * g + i) // 2, (3 * g + i) % 2 * half
            rest = rest + recve[e, 16:32, side : side + half].astype(F32)
        put(deep + i * half, (rest * row_scale[16:32] * gain).astype(BF16))

    long, short = nz // 2, nz - 1 - nz // 2
    d = 1 - 2 * core

    def zat(k):
        return lax.rem(z + k * d + 2 * nz, nz)

    def xat(k):
        return lax.rem(x + k * d + 2 * NX, NX)

    to_z = [{"seq": x * nz + zat(1)}, {"seq": x * nz + zat(-1)}]
    to_x = [{"seq": xat(j) * nz + z} for j in range(NX)]

    to_y = [{"exp": lax.rem(y + j * d + ny, ny) * 2 + core} for j in (1, -1)]
    sibling = {"exp": me + d}

    def columns(o):
        return pl.ds(zat(o) * NX, NX)

    def a1(j, back):
        u = z * NX + xat(-back)
        return remote(bufa.at[u], bufa.at[u], sa1.at[0], ra1.at[j - 1], to_x[j])

    def t1(j, back):
        part = tokb.at[core * ny + y, z * NX + xat(-back)]
        return remote(part, part, st1.at[0], rt1.at[j - 1], to_x[j])

    def a2(way, k, c, ahead=0):
        u = zat(-k - ahead if way == 0 else k + ahead) * NX + xat(-c)
        return remote(bufa.at[u], bufa.at[u], sa2.at[way], ra2.at[way, k, c], to_z[way])

    def t2(way, k, c, ahead=0):
        u = zat(-k - ahead if way == 0 else k + ahead) * NX + xat(-c)
        part = tokb.at[core * ny + y, u]
        return remote(part, part, st2.at[way], rt2.at[way, k, c], to_z[way])

    def tok_y(o, kind, back):
        part = tokb.at[core * ny + lax.rem(y - back * d + 2 * ny, ny), columns(o)]
        return remote(part, part, sy.at[0], ry.at[kind, o + nz], to_y[1 if kind == 1 else 0])

    def tok_core(o, whose):
        part = tokb.at[pl.ds(whose * ny, ny), columns(o)]
        return remote(part, part, ss.at[0], rs.at[o + nz], sibling)

    def y_spread(o):
        tok_y(o, 0, 0).start()
        tok_y(o, 1, 0).start()

    def y_forward(o):
        tok_y(o, 0, 1).wait_recv()
        tok_y(o, 2, 1).start()

    def y_share(o):
        tok_y(o, 1, -1).wait_recv()
        tok_y(o, 2, 2).wait_recv()
        tok_core(o, core).start()

    def b1(way, k):
        u = zat(-k if way == 0 else k) * NX + x
        return remote(bufb.at[u], bufb.at[u], sb1.at[way], rb1.at[way, k], to_z[way])

    def b1_arrived(way, k):
        u = zat(-k - 1 if way == 0 else k + 1) * NX + x
        return remote(bufb.at[u], bufb.at[u], sb1.at[way], rb1.at[way, k], to_z[way])

    def b2(o, kind):
        u = zat(o) * NX + (x if kind < 2 else xat(-1))
        where = to_x[NX - 1] if kind == 1 else to_x[1]
        return remote(bufb.at[u], bufb.at[u], sb2.at[0], rb2.at[kind, o + nz], where)

    def b2_arrived(o, kind):
        u = zat(o) * NX + xat((-1, 1, -2)[kind])
        where = to_x[NX - 1] if kind == 1 else to_x[1]
        return remote(bufb.at[u], bufb.at[u], sb2.at[0], rb2.at[kind, o + nz], where)

    def spread(o):
        b2(o, 0).start()
        b2(o, 1).start()

    def forward(o):
        b2_arrived(o, 0).wait_recv()
        b2(o, 2).start()

    def finish(o):
        b2_arrived(o, 1).wait_recv()
        b2_arrived(o, 2).wait_recv()
        tok_core(o, 1 - core).wait_recv()

    lanes = 16 * NX

    def compute(offsets):
        n = lanes * len(offsets)
        zs = [zat(o) for o in offsets]

        def stacked(buf, start, size):
            got = [
                buf[pl.ds(zz * NX, NX), :, start : start + size].reshape(lanes, size) for zz in zs
            ]
            return got[0] if len(got) == 1 else jnp.concatenate(got, axis=0)

        t = ((1,), (1,))
        main = dot(wbuf[:, 0:ka], stacked(bufa, 0, ka), t)
        main = main + dot(wbuf[:, ka:deep], stacked(bufb, 0, deep - ka), t)
        tail = stacked(bufb, deep - ka, quarter)
        lane = iota((2 * hidden, n), 1)
        rest = jnp.zeros((2 * hidden, n), F32)
        for g in range(4):
            one = dot(wbuf[:, g * quarter : (g + 1) * quarter], tail, t)
            rest = rest + jnp.where(lane % 16 // 4 == g, one, 0.0)
        span = NX * tokens
        line, key = iota((2 * lanes, span), 0), iota((2 * lanes, span), 1)
        r = line % 16
        want = jnp.where(line < lanes, r + 1, jnp.where(r >= 12, r + 5, -5))
        want = jnp.where(line % lanes // 16 == key // 16 % NX, want, -5).astype(F32)
        picked = [[], []]
        for zz in zs:
            tile = bufa[pl.ds(zz * NX, NX), :, ka : ka + 128].astype(F32).sum(axis=0)
            named = jnp.concatenate([tile[0:1], tile[1:2]], axis=1)
            pick = (jnp.abs(want - named) < 0.5).astype(F32).astype(BF16)
            for i in range(2):
                source = jnp.concatenate(
                    [
                        tokb[i * ny + t, pl.ds(zz * NX, NX)].reshape(NX * 16, width)
                        for t in range(ny)
                    ],
                    axis=0,
                )
                picked[i].append(dot(pick, source).astype(BF16))
        for i in range(2):
            w = wbuf[:, deep + i * width : deep + (i + 1) * width]
            main = main + dot(w, jnp.concatenate([p[0:lanes] for p in picked[i]], axis=0), t)
            rest = rest + dot(w, jnp.concatenate([p[lanes:] for p in picked[i]], axis=0), t)
        if n < 128:
            rest = jnp.concatenate([rest, jnp.zeros((2 * hidden, 128 - n), F32)], axis=1)
            main = jnp.concatenate([main, jnp.zeros((2 * hidden, 128 - n), F32)], axis=1)
        rest = sum([pltpu.roll(rest, 4 * g, 1) for g in range(1, 4)], rest)

        def gated(a):
            gate, up = a[0:hidden], a[hidden : 2 * hidden]
            return (gate / (1.0 + jnp.exp(-gate)) * up).astype(BF16)

        columns = acc.shape[1]
        l = iota((128, columns), 0)
        r = l % 16
        start = zs[0] * CAP if len(zs) == 1 else jnp.where(l < lanes, zs[0], zs[1]) * CAP
        start = start + l % lanes // 16 * (nz * CAP)
        n_at = iota((128, columns), 1)
        used = l < n
        p_main = ((n_at == start + r) & used).astype(F32).astype(BF16)
        p_rest = ((n_at == start + 16 + r % 4) & (r >= 12) & used).astype(F32).astype(BF16)
        acc[...] += dot(gated(main), p_main) + dot(gated(rest), p_rest)

    spread(0)
    for j in (1, 3, 2):
        t1(j, 0).start()
    for way in range(2):
        b1(way, 0).start()
        t2(way, 0, 0).start()
        a2(way, 0, 0).start()
    for j in (1, 3, 2):
        a1(j, 0).start()
    for j in (1, 3, 2):
        t1(j, j).wait_recv()
        for way in range(2):
            t2(way, 0, j).start()
    y_spread(0)
    for j in (1, 3, 2):
        a1(j, j).wait_recv()
        for way in range(2):
            a2(way, 0, j).start()
    for way, o in ((0, -1), (1, 1)):
        b1_arrived(way, 0).wait_recv()
        b1(way, 1).start()
        spread(o)
    for c in (0, 1, 3, 2):
        for way in range(2):
            t2(way, 0, c, 1).wait_recv()
            t2(way, 1, c).start()
    y_spread(-1)
    y_spread(1)
    forward(0)
    y_forward(0)

    def turn(t, first=False, both=True, ahead=(True, True)):
        ways = (0, 1) if both else (0,)
        for c in (0, 1, 3, 2):
            for way in ways:
                t2(way, t, c, 1).wait_recv()
                if ahead[way]:
                    t2(way, t + 1, c).start()
        for way in ways:
            y_spread(-t - 1 if way == 0 else t + 1)
        for way in ways:
            o = -t - 1 if way == 0 else t + 1
            b1_arrived(way, t).wait_recv()
            if ahead[way]:
                b1(way, t + 1).start()
            spread(o)
        for c in (0, 1, 3, 2):
            for way in range(2):
                a2(way, t - 1, c, 1).wait_recv()
                if way in ways:
                    a2(way, t, c).start()
        for o in (-t, t):
            forward(o)
            y_forward(o)
        if first:
            y_share(0)
            finish(0)
            compute([0])
        else:
            finish(1 - t)
            finish(t - 1)
            compute([1 - t, t - 1])
        y_share(-t)
        y_share(t)

    turn(1, first=True)

    @pl.loop(2, short - 1)
    def _(t):
        turn(t)

    turn(short - 1, ahead=(True, False))
    turn(long - 1, both=False, ahead=(False, False))
    forward(-long)
    y_forward(-long)
    finish(1 - long)
    finish(long - 1)
    y_share(-long)
    compute([1 - long, long - 1])
    for c in (0, 1, 3, 2):
        a2(0, long - 1, c, 1).wait_recv()
    finish(-long)
    compute([-long])
    out_ref[0] = acc[...].astype(BF16)

    def sent(buf, count, sem):
        span = buf.at[pl.ds(0, count)]
        remote(span, span, sem, ra1.at[0], to_z[0]).wait_send()

    sent(bufa, NX - 1, sa1.at[0])
    sent(tokb.at[0], NX - 1, st1.at[0])
    for way, count in ((0, long), (1, short)):
        sent(bufa, NX * count, sa2.at[way])
        sent(tokb.at[0], NX * count, st2.at[way])
    sent(tokb, 3, sy.at[0])
    sent(tokb, ny, ss.at[0])
    sent(bufb, long, sb1.at[0])
    sent(bufb, short, sb1.at[1])
    sent(bufb, 3 * nz, sb2.at[0])
    for c in pending:
        c.wait_send()
    for j, p in zpeers:
        remote(send2.at[p], recv2.at[p], s2.at[p], r2.at[p], {"seq": x * nz + p}).wait_send()

    @pl.when(me >= by_rows)
    def _():
        for t in range(ny - 1):
            raw_to(t).wait_send()

    @pl.when(me < by_rows)
    def _():
        for j, p in epeers:
            rows_to(j, p).wait_send()


def block(nz, ne, q, k, v, ld, sin, routes, gain, w_gate, w_up):
    tokens, width = q.shape
    heads, hd = ld.shape[0], sin.shape[1]
    rows = hd // nz
    _, hidden, depth = w_gate.shape
    units = NX * nz
    deep = depth - 2 * width
    ka = 2 * width
    kb = deep + deep // 4 - ka
    dma = pltpu.SemaphoreType.DMA
    vmem = pl.BlockSpec(memory_space=pltpu.VMEM)
    return pl.pallas_call(
        functools.partial(block_kernel, nz, ne),
        out_shape=(
            jax.ShapeDtypeStruct((1, hidden, units * CAP), BF16),
            jax.ShapeDtypeStruct((heads, rows // NX, hd), F32),
        ),
        in_specs=[pl.BlockSpec(memory_space=pl.ANY)] * 9,
        out_specs=(vmem, vmem),
        scratch_shapes=[
            pltpu.VMEM(q.shape, BF16),
            pltpu.VMEM(k.shape, BF16),
            pltpu.VMEM(v.shape, BF16),
            pltpu.VMEM(ld.shape, F32),
            pltpu.VMEM(sin.shape, F32),
            pltpu.VMEM(routes.shape, jnp.int32),
            pltpu.VMEM(gain.shape, F32),
            pltpu.VMEM((2 * hidden, depth), BF16),
            pltpu.VMEM((nz, heads * rows, hd), F32),
            pltpu.VMEM((nz, heads * rows, hd), BF16),
            pltpu.VMEM((nz, heads * rows, hd), BF16),
            pltpu.VMEM((nz, 1, hd), F32),
            pltpu.VMEM((NX, heads * rows + 8, hd), F32),
            pltpu.VMEM((nz, heads * rows, hd), BF16),
            pltpu.VMEM((nz, heads * rows, hd), BF16),
            pltpu.VMEM((nz, heads * rows, hd), F32),
            pltpu.VMEM((tokens, width), F32),
            pltpu.VMEM((ne, 32, width), BF16),
            pltpu.VMEM((ne, 32, width), BF16),
            pltpu.VMEM((ne, 1, hd), F32),
            pltpu.VMEM((ne // 2, 16, width), BF16),
            pltpu.VMEM((1, 16, width), BF16),
            pltpu.VMEM((units, 16, ka + 128), BF16),
            pltpu.VMEM((units, 16, kb), BF16),
            pltpu.VMEM((ne, units, 16, width), BF16),
            pltpu.VMEM((hidden, units * CAP), F32),
            dma((9,)),
            dma((nz,)),
            dma((nz,)),
            dma((nz,)),
            dma((nz,)),
            dma((NX,)),
            dma((NX,)),
            dma((nz,)),
            dma((nz,)),
            dma((ne,)),
            dma((ne,)),
            dma((ne,)),
            dma((ne,)),
            dma((ne // 2,)),
            dma((1,)),
            dma((1,)),
            dma((NX - 1,)),
            dma((1,)),
            dma((NX - 1,)),
            dma((2,)),
            dma((2, nz // 2, NX)),
            dma((2,)),
            dma((2, nz // 2, NX)),
            dma((2,)),
            dma((2, nz // 2)),
            dma((1,)),
            dma((3, 2 * nz)),
            dma((1,)),
            dma((3, 2 * nz)),
            dma((1,)),
            dma((2 * nz,)),
        ],
        compiler_params=pltpu.CompilerParams(
            collective_id=0, has_side_effects=True, vmem_limit_bytes=60 * 2**20
        ),
    )(q, k, v, ld, sin, routes, gain, w_gate, w_up)


def shards(nz, ne, queries, keys, values, log_decay, state_in, norm_gain, routes, w_gate, w_up):
    return block(
        nz, ne, queries, keys, values, log_decay, state_in, routes.T, norm_gain[None], w_gate, w_up
    )


def solution(mesh):
    placed = (
        P("seq", "exp"),
        P("seq", "exp"),
        P("seq", "exp"),
        P("exp", "seq"),
        P("exp", None, None),
        P(),
        P("seq", None),
        P("exp", "seq", None),
        P("exp", "seq", None),
    )
    return jax.shard_map(
        functools.partial(shards, mesh.shape["seq"] // NX, mesh.shape["exp"]),
        mesh=mesh,
        in_specs=placed,
        out_specs=(P("exp", "seq", None), P("exp", "seq", None)),
        check_vma=False,
    )
```
